32 devices in a mesh: rows: 8 (over y, x, core), cols: 4 (over z).
Axes of the slice: x: 2, y: 2, z: 4, core: 2. Of those that a mesh axis runs over, the one named last changes fastest.
Arguments:
- basis: bfloat16 [32768, 512], P(('rows', 'cols')), may hold values from -6 to 6
- blocks: bfloat16 [256, 8, 128, 128], P(('rows', 'cols')), may hold values from -0.1875 to 0.1875
- neighbours: int32 [256, 8], P(('rows', 'cols')), may hold values from 0 to 255, as said below
- counts: int32 [256], P(('rows', 'cols')), may hold values from 3 to 8
- rotation: bfloat16 [512, 256], replicated, may hold values from -0.25 to 0.25
- ritz_values: float32 [256], replicated, may hold values from -2 to 2
Outputs:
- ritz: bfloat16 [32768, 256], P(('rows', 'cols'))
- ritz_image: bfloat16 [32768, 256], P(('rows', 'cols'))
- gram: float32 [512, 512], P('rows')
- projected: float32 [512, 512], P('rows')
- res_norm: float32 [256], replicated
The draws below stay inside these ranges and needn't reach their ends.
Inputs may be any that keep to these rules, and one draw needn't show every extreme that they name: `neighbours`: every entry of row block b lies among the blocks of b's device and the one block just before and just after them: from 8 * (b // 8) - 1 to 8 * (b // 8) + 8; slot 0 is b itself; entries may repeat; entries at slots from counts[b] on are padding. `counts`: at least three slots are live.
All inputs are finite; a program needn't handle non-finite values.
Results may differ from the reference program's by a relative error of at most 0.015.
Values may be sent and summed in bfloat16 or wider, within the bound.
A program may use at most 64 MiB of HBM per device.

```python
import jax
import jax.numpy as jnp
from jax import lax

BS = 128
NB = 8
NNB = 8
K = 512
M = 256
NBLK = 256
ROWS = 32768


def draw_neighbours(key, part):
    blk = jnp.arange(NBLK, dtype=jnp.int32)
    owner = blk // NB
    local = blk % NB
    lower = owner * NB - 1
    offsets = jax.random.randint(jax.random.fold_in(key, 7), (NBLK, NNB), 0, NB + 2).astype(jnp.int32)
    entry = lower[:, None] + offsets
    entry = entry.at[:, 0].set(blk)
    entry = entry.at[:, 1].set(jnp.where(local == 0, lower, entry[:, 1]))
    entry = entry.at[:, 2].set(jnp.where(local == NB - 1, lower + NB + 1, entry[:, 2]))
    return jnp.clip(entry, 0, NBLK - 1).astype(jnp.int32)


def with_ends(entries, own_key, low, top_value):
    dims = entries.shape
    place = [jax.random.randint(jax.random.fold_in(own_key, axis), (), 0, dims[axis]) for axis in range(len(dims))]
    entries = entries.at[tuple(place)].set(low)
    longest = dims.index(max(dims))
    place[longest] = (place[longest] + 1) % dims[longest]
    return entries.at[tuple(place)].set(top_value)


def raised(values, stream_key, source, target, blocks, factor):
    def block_of(dim):
        return (jnp.arange(values.shape[dim]) // (values.shape[dim] // blocks)).reshape((-1,) + (1,) * (values.ndim - 1 - dim))

    one_side = jax.random.permutation(stream_key, blocks)[block_of(target)]
    far = (block_of(target) + blocks // 2) % blocks
    return jnp.where((block_of(source) == one_side) | (block_of(source) == far), factor * values, values)


def block_scale(rng, extent, shards, smallest, high):
    loudness = 1.0
    for position, blocks in shards:
        draws = jax.random.uniform(jax.random.fold_in(jax.random.fold_in(rng, 6), position), (blocks,), jnp.float32, smallest / len(shards), high / len(shards))
        loudness = loudness * jnp.repeat(jnp.exp(draws), extent[position] // blocks).reshape((-1,) + (1,) * (len(extent) - 1 - position))
    return loudness


def centred(rng, dims, scale, limit, shards=(), kind=jnp.bfloat16):
    level = block_scale(rng, dims, shards, -0.22, 0.18) if shards else 1.0
    drawn = jax.random.normal(rng, dims, jnp.float32) * scale * level
    return jnp.minimum(jnp.maximum(drawn, -limit), limit).astype(kind)


def gaussian_with(stream_key, shape, scale, bound, cuts, heavy, kind=jnp.bfloat16):
    entries = scale * jax.random.normal(stream_key, shape, jnp.float32)
    if cuts:
        entries = entries * block_scale(stream_key, shape, cuts, -0.22, 0.18)
    return jnp.clip(raised(entries, jax.random.fold_in(stream_key, 3), *heavy), -bound, bound).astype(kind)


def setup_inputs(seed: int = 0) -> dict:
    key_of = jax.random.split(jax.random.key(seed), 7)
    basis = gaussian_with(key_of[0], (ROWS, K), 1.0, 6.0, ((0, 32),), (0, 1, 32, 2.75))
    blocks = centred(key_of[1], (NBLK, NNB, BS, BS), (BS * NNB) ** -0.5, 0.1875, ((0, 32),))
    neighbours = draw_neighbours(jax.random.fold_in(key_of[6], 71), 0)
    counts = with_ends(jax.random.randint(key_of[3], (NBLK,), 3, NNB + 1), jax.random.fold_in(key_of[3], 1), 3, NNB).astype(jnp.int32)
    rotation = centred(key_of[4], (K, M), K ** -0.5, 0.25)
    ritz_values = jnp.clip(jax.random.uniform(key_of[5], (M,), jnp.float32, -2.0, 2.0), -2.0, 2.0)
    return dict(basis=basis, blocks=blocks, neighbours=neighbours, counts=counts, rotation=rotation, ritz_values=ritz_values)


def block_rows(args):
    held, index, vb = (args[0], args[1], args[2])
    total = jnp.zeros((held.shape[0], BS, K), jnp.float32)
    for slot in range(NNB):
        picked = vb[index[:, slot]].astype(jnp.float32)
        total = total + jnp.einsum('brs,bsk->brk', held[:, slot].astype(jnp.float32), picked)
    return total.astype(jnp.bfloat16)

def reference(basis, blocks, neighbours, counts, rotation, ritz_values):
    vb = basis.reshape(NBLK, BS, K)
    live = jnp.arange(NNB, dtype=jnp.int32)[None, :] < counts[:, None]
    masked = jnp.where(live[:, :, None, None], blocks, jnp.zeros_like(blocks))
    groups = NBLK // NB
    image = lax.map(lambda pair: block_rows((pair[0], pair[1], vb)), (masked.reshape(groups, NB, NNB, BS, BS), neighbours.reshape(groups, NB, NNB)))
    image = image.reshape(ROWS, K)
    gram = jnp.dot(basis.T, basis, preferred_element_type=jnp.float32) / ROWS
    projected = jnp.dot(basis.T, image, preferred_element_type=jnp.float32) / ROWS
    ritz_full = jnp.dot(basis, rotation, preferred_element_type=jnp.float32)
    image_full = jnp.dot(image, rotation, preferred_element_type=jnp.float32)
    resid = image_full - ritz_values[None, :] * ritz_full
    res_norm = jnp.sqrt(lax.optimization_barrier(jnp.sum(resid * resid, axis=0)) / ROWS)
    return (ritz_full.astype(jnp.bfloat16), image_full.astype(jnp.bfloat16), gram, projected, res_norm)
```

```python
import functools

import jax
import jax.numpy as jnp
from jax import lax
from jax.experimental import pallas as pl
from jax.experimental.pallas import tpu as pltpu
from jax.sharding import PartitionSpec as P


def extended(block, sides, width):
    for axis, dim in sides:
        count = lax.axis_size(axis)
        forward = [(i, i + 1) for i in range(count - 1)]
        backward = [(target, source) for source, target in forward]
        low = lax.ppermute(
            lax.slice_in_dim(block, block.shape[dim] - width, None, axis=dim), axis, forward
        )
        high = lax.ppermute(lax.slice_in_dim(block, 0, width, axis=dim), axis, backward)
        block = jnp.concatenate([low, block, high], axis=dim)
    return block


def general_body(basis, blocks, neighbours, counts, rotation, ritz_values):
    count_blocks = blocks.shape[0]
    slots = blocks.shape[1]
    size_block = blocks.shape[2]
    width = basis.shape[1]
    devices = lax.axis_size("rows") * lax.axis_size("cols")
    rows_total = basis.shape[0] * devices
    first = lax.axis_index(("rows", "cols")) * count_blocks - 1
    local_index = neighbours - first
    live = jnp.arange(slots, dtype=jnp.int32)[None, :] < counts[:, None]
    masked = jnp.where(live[:, :, None, None], blocks, jnp.zeros_like(blocks))
    total = jnp.zeros((count_blocks, size_block, width), jnp.float32)
    own = basis.reshape(count_blocks, size_block, width)
    inside = (local_index >= 1) & (local_index <= count_blocks)
    for slot in range(slots):
        picked = own[jnp.clip(local_index[:, slot] - 1, 0, count_blocks - 1)]
        held = jnp.where(
            inside[:, slot][:, None, None], masked[:, slot], jnp.zeros_like(masked[:, slot])
        )
        total = total + jnp.einsum("brs,bsk->brk", held, picked, preferred_element_type=jnp.float32)
    padded = extended(basis, ((("rows", "cols"), 0),), size_block)
    lower_rows = padded[:size_block]
    upper_rows = padded[-size_block:]
    zero_block = jnp.zeros_like(masked)
    below = jnp.sum(jnp.where((local_index == 0)[:, :, None, None], masked, zero_block), axis=1)
    above = jnp.sum(
        jnp.where((local_index == count_blocks + 1)[:, :, None, None], masked, zero_block), axis=1
    )
    total = total + jnp.einsum("brs,sk->brk", below, lower_rows, preferred_element_type=jnp.float32)
    total = total + jnp.einsum("brs,sk->brk", above, upper_rows, preferred_element_type=jnp.float32)
    image = total.reshape(basis.shape[0], width).astype(jnp.bfloat16)
    joined = jnp.concatenate([basis, image], axis=1)
    partial_rows = lax.psum_scatter(
        jnp.dot(basis.T, joined, preferred_element_type=jnp.float32) / rows_total,
        "rows",
        scatter_dimension=0,
        tiled=True,
    )
    both = lax.psum(partial_rows.astype(jnp.bfloat16), "cols").astype(jnp.float32)
    gram = both[:, :width]
    projected = both[:, width:]
    ritz_full = jnp.dot(basis, rotation, preferred_element_type=jnp.float32)
    image_full = jnp.dot(image, rotation, preferred_element_type=jnp.float32)
    resid = image_full - ritz_values[None, :] * ritz_full
    squares = lax.psum(jnp.sum(resid * resid, axis=0), ("rows", "cols"))
    res_norm = jnp.sqrt(squares / rows_total)
    return (
        ritz_full.astype(jnp.bfloat16),
        image_full.astype(jnp.bfloat16),
        gram,
        projected,
        res_norm,
    )


BF16, F32 = jnp.bfloat16, jnp.float32


def dot(a, b):
    return jnp.dot(a, b, preferred_element_type=F32)


def fold(x):
    return jnp.sum(x.reshape(x.shape[0] // 8, 8, x.shape[1]), axis=0)


def kernel(
    sizes, nbr, cnt, basis_hbm, blocks_hbm, rot, vals,
    ritz_hbm, rimg_hbm, gram_out, proj_out, res_out,
    own, blk, mat_in, mat_halo, halo, acc, image, bt, rfull, ritz_v, rimg_v,
    half, core_send, core_recv, part, plane_send, plane_recv,
    z_send, z_recv, gat, sq_own, sq_core, sq_plane, sq_z,
    local_sem, halo_ss, halo_rs, core_ss, core_rs, plane_ss, plane_rs,
    zs_ss, zs_rs, za_ss, za_rs,
):
    nb, nnb, bs, k, m, R, Z = sizes
    Q = R // 2
    rows = nb * bs
    chunk = k // R
    piece = chunk // Z
    rows_total = rows * R * Z
    r = lax.axis_index("rows")
    z = lax.axis_index("cols")
    c = lax.rem(r, 2)
    q = r // 2
    me = r * Z + z
    first = me * nb - 1

    def at(index):
        return (index // Z, lax.rem(index, Z))

    ahead = at(lax.rem(me + 1, R * Z))
    behind = at(lax.rem(me + R * Z - 1, R * Z))
    mate = (q * 2 + 1 - c, z)
    plane_q = [lax.rem(q + d, Q) for d in range(1, Q)]
    plane = [(p * 2 + c, z) for p in plane_q]
    line_z = [lax.rem(z + d, Z) for d in range(1, Z)]
    line = [(r, p) for p in line_z]

    get_basis = pltpu.make_async_copy(basis_hbm, own, local_sem.at[0])
    get_basis.start()
    get_blocks = pltpu.make_async_copy(blocks_hbm, blk, local_sem.at[1])
    get_blocks.start()

    barrier = pltpu.get_barrier_semaphore()
    peers = [ahead, behind, mate] + plane + line
    for peer in peers:
        pl.semaphore_signal(barrier, inc=1, device_id=peer, device_id_type=pl.DeviceIdType.MESH)
    pl.semaphore_wait(barrier, len(peers))

    sends = []

    def remote(src, dst, ss, rs, to):
        copy = pltpu.make_async_remote_copy(
            src_ref=src, dst_ref=dst, send_sem=ss, recv_sem=rs,
            device_id=to, device_id_type=pl.DeviceIdType.MESH,
        )
        copy.start()
        sends.append(copy)
        return copy

    halo_copies = [
        remote(basis_hbm.at[pl.ds(rows - bs, bs)], halo.at[pl.ds(0, bs)],
               halo_ss.at[0], halo_rs.at[0], ahead),
        remote(basis_hbm.at[pl.ds(0, bs)], halo.at[pl.ds(bs, bs)],
               halo_ss.at[1], halo_rs.at[1], behind),
    ]

    get_basis.wait()
    for i in range(Q):
        turned = own[:, i * 2 * chunk:(i + 1) * 2 * chunk].T
        for side in range(2):
            bt[side, pl.ds(i * chunk, chunk), :] = turned[side * chunk:(side + 1) * chunk]

    def core_phase(which, right):
        core_send[which] = dot(bt[1 - c], right[...]).astype(BF16)
        copy = remote(core_send.at[which], core_recv.at[which], core_ss.at[which],
                      core_rs.at[which], mate)
        half[which] = dot(bt[c], right[...])
        return copy

    def plane_phase(which, core_copy):
        core_copy.wait_recv()
        total = half[which] + core_recv[which].astype(F32)
        half[which] = total
        plane_send[which] = total.astype(BF16).reshape(Q, chunk, k)
        return [
            remote(plane_send.at[which, plane_q[d]], plane_recv.at[which, d],
                   plane_ss.at[which, d], plane_rs.at[which, d], plane[d])
            for d in range(Q - 1)
        ]

    def line_phase(which, copies):
        total = half[which, pl.ds(pl.multiple_of(q * chunk, chunk), chunk), :]
        for d, copy in enumerate(copies):
            copy.wait_recv()
            total = total + plane_recv[which, d].astype(F32)
        part[which] = total
        z_send[which] = total.astype(BF16).reshape(Z, piece, k)
        return [
            remote(z_send.at[which, line_z[d]], z_recv.at[which, d],
                   zs_ss.at[which, d], zs_rs.at[which, d], line[d])
            for d in range(Z - 1)
        ]

    def gather_phase(which, copies):
        total = part[which, pl.ds(pl.multiple_of(z * piece, piece), piece), :]
        for d, copy in enumerate(copies):
            copy.wait_recv()
            total = total + z_recv[which, d].astype(F32)
        gat[which, z] = total.astype(BF16)
        return [
            remote(gat.at[which, z], gat.at[which, z],
                   za_ss.at[which, d], za_rs.at[which, d], line[d])
            for d in range(Z - 1)
        ]

    def finish(which, copies, out):
        for copy in copies:
            copy.wait_recv()
        out[...] = gat[which].astype(F32).reshape(chunk, k) / rows_total

    gram_core = core_phase(0, own)

    rfull[...] = dot(own[...], rot[...])
    ritz_v[...] = rfull[...].astype(BF16)
    put_ritz = pltpu.make_async_copy(ritz_v, ritz_hbm, local_sem.at[2])
    put_ritz.start()

    get_blocks.wait()

    @pl.loop(0, nb)
    def _(b):
        n = cnt[b]
        spot = [jnp.where(j < n, nbr[b, j] - first, -1) for j in range(nnb)]
        tiles = [blk[b, j] for j in range(nnb)]
        there = pl.ds(pl.multiple_of(b * bs, bs), bs)
        for s in range(nb + 2):
            total = jnp.zeros((bs, bs), BF16)
            for j in range(nnb):
                weight = jnp.where(spot[j] == s, 1.0, 0.0).astype(F32)
                total = total + tiles[j] * jnp.full((bs, bs), weight, F32).astype(BF16)
            if s == 0:
                mat_halo[there, 0:bs] = total
            elif s == nb + 1:
                mat_halo[there, bs:2 * bs] = total
            else:
                mat_in[there, (s - 1) * bs:s * bs] = total

    gram_plane = plane_phase(0, gram_core)

    step = min(rows, 2 * bs)

    @pl.loop(0, rows // step)
    def _(i):
        there = pl.ds(pl.multiple_of(i * step, step), step)
        acc[there, :] = dot(mat_in[there, :], own[...])

    gram_line = line_phase(0, gram_plane)

    for copy in halo_copies:
        copy.wait_recv()

    @pl.loop(0, rows // step)
    def _(i):
        there = pl.ds(pl.multiple_of(i * step, step), step)
        image[there, :] = (acc[there, :] + dot(mat_halo[there, :], halo[...])).astype(BF16)

    proj_core = core_phase(1, image)
    gram_gather = gather_phase(0, gram_line)

    sq_own[...] = jnp.zeros_like(sq_own)

    @pl.loop(0, rows // step)
    def _(i):
        there = pl.ds(pl.multiple_of(i * step, step), step)
        full = dot(image[there, :], rot[...])
        rimg_v[there, :] = full.astype(BF16)
        resid = full - vals[...] * rfull[there, :]
        sq_own[...] += fold(resid * resid)

    put_rimg = pltpu.make_async_copy(rimg_v, rimg_hbm, local_sem.at[3])
    put_rimg.start()
    sq_copy = remote(sq_own, sq_core, core_ss.at[2], core_rs.at[2], mate)

    proj_plane = plane_phase(1, proj_core)
    sq_copy.wait_recv()
    sq_plane[q] = sq_own[...] + sq_core[...]
    sq_copies = [
        remote(sq_plane.at[q], sq_plane.at[q], plane_ss.at[2, d], plane_rs.at[2, d], plane[d])
        for d in range(Q - 1)
    ]
    finish(0, gram_gather, gram_out)
    proj_line = line_phase(1, proj_plane)
    for copy in sq_copies:
        copy.wait_recv()
    sq_z[z] = jnp.sum(sq_plane[...], axis=0)
    sq_copies = [
        remote(sq_z.at[z], sq_z.at[z], za_ss.at[2, d], za_rs.at[2, d], line[d])
        for d in range(Z - 1)
    ]
    proj_gather = gather_phase(1, proj_line)
    for copy in sq_copies:
        copy.wait_recv()
    squares = jnp.sum(jnp.sum(sq_z[...], axis=0), axis=0, keepdims=True)
    res_out[...] = jnp.sqrt(squares / rows_total)
    finish(1, proj_gather, proj_out)
    for copy in sends:
        copy.wait_send()
    put_ritz.wait()
    put_rimg.wait()


def fused_body(basis, blocks, neighbours, counts, rotation, ritz_values):
    R, Z = lax.axis_size("rows"), lax.axis_size("cols")
    nb, nnb, bs, _ = blocks.shape
    rows, k = basis.shape
    m = rotation.shape[1]
    Q, chunk, piece = R // 2, k // R, k // R // Z
    vmem = pltpu.VMEM
    dma = pltpu.SemaphoreType.DMA
    any_spec = pl.BlockSpec(memory_space=pl.ANY)
    smem_spec = pl.BlockSpec(memory_space=pltpu.SMEM)
    vmem_spec = pl.BlockSpec(memory_space=pltpu.VMEM)
    ritz, rimg, gram, proj, res = pl.pallas_call(
        functools.partial(kernel, (nb, nnb, bs, k, m, R, Z)),
        out_shape=(
            jax.ShapeDtypeStruct((rows, m), BF16),
            jax.ShapeDtypeStruct((rows, m), BF16),
            jax.ShapeDtypeStruct((chunk, k), F32),
            jax.ShapeDtypeStruct((chunk, k), F32),
            jax.ShapeDtypeStruct((1, m), F32),
        ),
        in_specs=[smem_spec, smem_spec, any_spec, any_spec, vmem_spec, vmem_spec],
        out_specs=(any_spec, any_spec, vmem_spec, vmem_spec, vmem_spec),
        scratch_shapes=[
            vmem((rows, k), BF16),
            vmem((nb, nnb, bs, bs), BF16),
            vmem((rows, nb * bs), BF16),
            vmem((rows, 2 * bs), BF16),
            vmem((2 * bs, k), BF16),
            vmem((rows, k), F32),
            vmem((rows, k), BF16),
            vmem((2, k // 2, rows), BF16),
            vmem((rows, m), F32),
            vmem((rows, m), BF16),
            vmem((rows, m), BF16),
            vmem((2, k // 2, k), F32),
            vmem((2, k // 2, k), BF16),
            vmem((2, k // 2, k), BF16),
            vmem((2, chunk, k), F32),
            vmem((2, Q, chunk, k), BF16),
            vmem((2, Q - 1, chunk, k), BF16),
            vmem((2, Z, piece, k), BF16),
            vmem((2, Z - 1, piece, k), BF16),
            vmem((2, Z, piece, k), BF16),
            vmem((8, m), F32),
            vmem((8, m), F32),
            vmem((Q, 8, m), F32),
            vmem((Z, 8, m), F32),
            dma((4,)),
            dma((2,)),
            dma((2,)),
            dma((3,)),
            dma((3,)),
            dma((3, Q - 1)),
            dma((3, Q - 1)),
            dma((2, Z - 1)),
            dma((2, Z - 1)),
            dma((3, Z - 1)),
            dma((3, Z - 1)),
        ],
        compiler_params=pltpu.CompilerParams(
            collective_id=0, has_side_effects=True, vmem_limit_bytes=40 * 1024 * 1024
        ),
        name="davidson_step",
    )(neighbours, counts, basis, blocks, rotation, ritz_values.reshape(1, m))
    return ritz, rimg, gram, proj, res.reshape(m)


def body(basis, blocks, neighbours, counts, rotation, ritz_values):
    R, Z = lax.axis_size("rows"), lax.axis_size("cols")
    k = basis.shape[1]
    even = R % 4 == 0 and Z > 1 and k % (16 * R * Z) == 0 and (2 * k // R) % 128 == 0
    chosen = fused_body if even else general_body
    return chosen(basis, blocks, neighbours, counts, rotation, ritz_values)


def solution(mesh):
    return jax.shard_map(
        body,
        mesh=mesh,
        in_specs=(
            P(("rows", "cols"), None),
            P(("rows", "cols"), None, None, None),
            P(("rows", "cols"), None),
            P(("rows", "cols")),
            P(),
            P(),
        ),
        out_specs=(
            P(("rows", "cols"), None),
            P(("rows", "cols"), None),
            P("rows", None),
            P("rows", None),
            P(),
        ),
        check_vma=False,
    )
```

```python
import functools

import jax
import jax.numpy as jnp
from jax import lax
from jax.experimental import pallas as pl
from jax.experimental.pallas import tpu as pltpu
from jax.sharding import PartitionSpec as P


def extended(block, sides, width):
    for axis, dim in sides:
        count = lax.axis_size(axis)
        forward = [(i, i + 1) for i in range(count - 1)]
        backward = [(target, source) for source, target in forward]
        low = lax.ppermute(
            lax.slice_in_dim(block, block.shape[dim] - width, None, axis=dim), axis, forward
        )
        high = lax.ppermute(lax.slice_in_dim(block, 0, width, axis=dim), axis, backward)
        block = jnp.concatenate([low, block, high], axis=dim)
    return block


def general_body(basis, blocks, neighbours, counts, rotation, ritz_values):
    count_blocks = blocks.shape[0]
    slots = blocks.shape[1]
    size_block = blocks.shape[2]
    width = basis.shape[1]
    devices = lax.axis_size("rows") * lax.axis_size("cols")
    rows_total = basis.shape[0] * devices
    first = lax.axis_index(("rows", "cols")) * count_blocks - 1
    local_index = neighbours - first
    live = jnp.arange(slots, dtype=jnp.int32)[None, :] < counts[:, None]
    masked = jnp.where(live[:, :, None, None], blocks, jnp.zeros_like(blocks))
    total = jnp.zeros((count_blocks, size_block, width), jnp.float32)
    own = basis.reshape(count_blocks, size_block, width)
    inside = (local_index >= 1) & (local_index <= count_blocks)
    for slot in range(slots):
        picked = own[jnp.clip(local_index[:, slot] - 1, 0, count_blocks - 1)]
        held = jnp.where(
            inside[:, slot][:, None, None], masked[:, slot], jnp.zeros_like(masked[:, slot])
        )
        total = total + jnp.einsum("brs,bsk->brk", held, picked, preferred_element_type=jnp.float32)
    padded = extended(basis, ((("rows", "cols"), 0),), size_block)
    lower_rows = padded[:size_block]
    upper_rows = padded[-size_block:]
    zero_block = jnp.zeros_like(masked)
    below = jnp.sum(jnp.where((local_index == 0)[:, :, None, None], masked, zero_block), axis=1)
    above = jnp.sum(
        jnp.where((local_index == count_blocks + 1)[:, :, None, None], masked, zero_block), axis=1
    )
    total = total + jnp.einsum("brs,sk->brk", below, lower_rows, preferred_element_type=jnp.float32)
    total = total + jnp.einsum("brs,sk->brk", above, upper_rows, preferred_element_type=jnp.float32)
    image = total.reshape(basis.shape[0], width).astype(jnp.bfloat16)
    joined = jnp.concatenate([basis, image], axis=1)
    partial_rows = lax.psum_scatter(
        jnp.dot(basis.T, joined, preferred_element_type=jnp.float32) / rows_total,
        "rows",
        scatter_dimension=0,
        tiled=True,
    )
    both = lax.psum(partial_rows.astype(jnp.bfloat16), "cols").astype(jnp.float32)
    gram = both[:, :width]
    projected = both[:, width:]
    ritz_full = jnp.dot(basis, rotation, preferred_element_type=jnp.float32)
    image_full = jnp.dot(image, rotation, preferred_element_type=jnp.float32)
    resid = image_full - ritz_values[None, :] * ritz_full
    squares = lax.psum(jnp.sum(resid * resid, axis=0), ("rows", "cols"))
    res_norm = jnp.sqrt(squares / rows_total)
    return (
        ritz_full.astype(jnp.bfloat16),
        image_full.astype(jnp.bfloat16),
        gram,
        projected,
        res_norm,
    )


BF16, F32 = jnp.bfloat16, jnp.float32
PARTS = 2
SQ = 2 * PARTS


def dot(a, b):
    return jnp.dot(a, b, preferred_element_type=F32)


def fold(x):
    return jnp.sum(x.reshape(x.shape[0] // 8, 8, x.shape[1]), axis=0)


def kernel(
    sizes, nbr, cnt, basis_hbm, blocks_hbm, rot_hbm, vals_hbm,
    ritz_hbm, sums_out, res_out,
    rot, vals,
    own, blk, mat_in, mat_halo, halo, acc, image, bt, rfull, ritz_v, rimg_v,
    half, core_send, core_recv, part, plane_send, plane_recv,
    z_send, z_recv, gat, sq_own, sq_core, sq_plane, sq_z,
    local_sem, halo_ss, halo_rs, core_ss, core_rs, plane_ss, plane_rs,
    zs_ss, zs_rs, za_ss, za_rs,
):
    nb, nnb, bs, k, m, R, Z = sizes
    Q = R // 2
    rows = nb * bs
    chunk = k // R
    piece = chunk // Z
    rows_total = rows * R * Z
    r = lax.axis_index("rows")
    z = lax.axis_index("cols")
    c = lax.rem(r, 2)
    q = r // 2
    me = r * Z + z
    first = me * nb - 1

    def at(index):
        return (index // Z, lax.rem(index, Z))

    ahead = at(lax.rem(me + 1, R * Z))
    behind = at(lax.rem(me + R * Z - 1, R * Z))
    mate = (q * 2 + 1 - c, z)
    plane_q = [lax.rem(q + d, Q) for d in range(1, Q)]
    plane = [(p * 2 + c, z) for p in plane_q]
    line_z = [lax.rem(z + d, Z) for d in range(1, Z)]
    line = [(r, p) for p in line_z]

    get_basis = pltpu.make_async_copy(basis_hbm, own, local_sem.at[0])
    get_basis.start()
    get_blocks = pltpu.make_async_copy(blocks_hbm, blk, local_sem.at[1])
    get_blocks.start()
    get_rot = pltpu.make_async_copy(rot_hbm, rot, local_sem.at[4])
    get_rot.start()
    get_vals = pltpu.make_async_copy(vals_hbm, vals, local_sem.at[5])
    get_vals.start()

    barrier = pltpu.get_barrier_semaphore()
    peers = [ahead, behind, mate] + plane + line
    for peer in peers:
        pl.semaphore_signal(barrier, inc=1, device_id=peer, device_id_type=pl.DeviceIdType.MESH)
    pl.semaphore_wait(barrier, len(peers))

    sends = []

    def remote(src, dst, ss, rs, to):
        copy = pltpu.make_async_remote_copy(
            src_ref=src, dst_ref=dst, send_sem=ss, recv_sem=rs,
            device_id=to, device_id_type=pl.DeviceIdType.MESH,
        )
        copy.start()
        sends.append(copy)
        return copy

    halo_copies = [
        remote(basis_hbm.at[pl.ds(rows - bs, bs)], halo.at[pl.ds(0, bs)],
               halo_ss.at[0], halo_rs.at[0], ahead),
        remote(basis_hbm.at[pl.ds(0, bs)], halo.at[pl.ds(bs, bs)],
               halo_ss.at[1], halo_rs.at[1], behind),
    ]

    get_basis.wait()
    for i in range(Q):
        turned = own[:, i * 2 * chunk:(i + 1) * 2 * chunk].T
        for side in range(2):
            bt[side, pl.ds(i * chunk, chunk), :] = turned[side * chunk:(side + 1) * chunk]

    wide = k // PARTS

    def columns(which):
        return pl.ds((which % PARTS) * wide, wide)

    def core_phase(which, right):
        core_send[which] = dot(bt[1 - c], right[:, columns(which)]).astype(BF16)
        copy = remote(core_send.at[which], core_recv.at[which], core_ss.at[which],
                      core_rs.at[which], mate)
        return copy

    def own_half(which, right):
        half[which] = dot(bt[c], right[:, columns(which)])

    def plane_phase(which, core_copy):
        core_copy.wait_recv()
        total = half[which] + core_recv[which].astype(F32)
        half[which] = total
        plane_send[which] = total.astype(BF16).reshape(Q, chunk, wide)
        return [
            remote(plane_send.at[which, plane_q[d]], plane_recv.at[which, d],
                   plane_ss.at[which, d], plane_rs.at[which, d], plane[d])
            for d in range(Q - 1)
        ]

    def line_phase(which, copies):
        total = half[which, pl.ds(pl.multiple_of(q * chunk, chunk), chunk), :]
        for d, copy in enumerate(copies):
            copy.wait_recv()
            total = total + plane_recv[which, d].astype(F32)
        part[which] = total
        z_send[which] = total.astype(BF16).reshape(Z, piece, wide)
        return [
            remote(z_send.at[which, line_z[d]], z_recv.at[which, d],
                   zs_ss.at[which, d], zs_rs.at[which, d], line[d])
            for d in range(Z - 1)
        ]

    def gather_phase(which, copies):
        total = part[which, pl.ds(pl.multiple_of(z * piece, piece), piece), :]
        for d, copy in enumerate(copies):
            copy.wait_recv()
            total = total + z_recv[which, d].astype(F32)
        gat[which, z] = total.astype(BF16)
        return [
            remote(gat.at[which, z], gat.at[which, z],
                   za_ss.at[which, d], za_rs.at[which, d], line[d])
            for d in range(Z - 1)
        ]

    def finish(which, copies):
        for copy in copies:
            copy.wait_recv()
        sums_out[which // PARTS, :, columns(which)] = (
            gat[which].astype(F32).reshape(chunk, wide) / rows_total
        )

    gram = range(PARTS)
    proj = range(PARTS, 2 * PARTS)

    gram_core = [core_phase(u, own) for u in gram]
    for u in gram:
        own_half(u, own)

    get_rot.wait()
    rfull[...] = dot(own[...], rot[...])
    ritz_v[...] = rfull[...].astype(BF16)
    put_ritz = pltpu.make_async_copy(ritz_v, ritz_hbm.at[0], local_sem.at[2])
    put_ritz.start()

    get_blocks.wait()

    @pl.loop(0, nb)
    def _(b):
        n = cnt[b]
        spot = [jnp.where(j < n, nbr[b, j] - first, -1) for j in range(nnb)]
        tiles = [blk[b, j] for j in range(nnb)]
        there = pl.ds(pl.multiple_of(b * bs, bs), bs)
        for s in range(nb + 2):
            total = jnp.zeros((bs, bs), BF16)
            for j in range(nnb):
                weight = jnp.where(spot[j] == s, 1.0, 0.0).astype(F32)
                total = total + tiles[j] * jnp.full((bs, bs), weight, F32).astype(BF16)
            if s == 0:
                mat_halo[there, 0:bs] = total
            elif s == nb + 1:
                mat_halo[there, bs:2 * bs] = total
            else:
                mat_in[there, (s - 1) * bs:s * bs] = total

    gram_plane = [plane_phase(u, gram_core[u]) for u in gram]

    step = min(rows, 2 * bs)

    @pl.loop(0, rows // step)
    def _(i):
        there = pl.ds(pl.multiple_of(i * step, step), step)
        acc[there, :] = dot(mat_in[there, :], own[...])

    gram_line = [line_phase(u, gram_plane[u]) for u in gram]

    for copy in halo_copies:
        copy.wait_recv()

    @pl.loop(0, rows // step)
    def _(i):
        there = pl.ds(pl.multiple_of(i * step, step), step)
        image[there, :] = (acc[there, :] + dot(mat_halo[there, :], halo[...])).astype(BF16)

    proj_core = [core_phase(u, image) for u in proj]
    for u in proj:
        own_half(u, image)
    proj_plane = [plane_phase(u, copy) for u, copy in zip(proj, proj_core)]
    get_vals.wait()

    sq_own[...] = jnp.zeros_like(sq_own)

    @pl.loop(0, rows // step)
    def _(i):
        there = pl.ds(pl.multiple_of(i * step, step), step)
        full = dot(image[there, :], rot[...])
        rimg_v[there, :] = full.astype(BF16)
        resid = full - vals[...] * rfull[there, :]
        sq_own[...] += fold(resid * resid)

    put_rimg = pltpu.make_async_copy(rimg_v, ritz_hbm.at[1], local_sem.at[3])
    put_rimg.start()
    sq_copy = remote(sq_own, sq_core, core_ss.at[SQ], core_rs.at[SQ], mate)

    gram_gather = [gather_phase(u, gram_line[u]) for u in gram]
    proj_line = [line_phase(u, copies) for u, copies in zip(proj, proj_plane)]
    sq_copy.wait_recv()
    sq_plane[q] = sq_own[...] + sq_core[...]
    sq_copies = [
        remote(sq_plane.at[q], sq_plane.at[q], plane_ss.at[SQ, d], plane_rs.at[SQ, d], plane[d])
        for d in range(Q - 1)
    ]
    for u in gram:
        finish(u, gram_gather[u])
    proj_gather = [gather_phase(u, copies) for u, copies in zip(proj, proj_line)]
    for copy in sq_copies:
        copy.wait_recv()
    sq_z[z] = jnp.sum(sq_plane[...], axis=0)
    sq_copies = [
        remote(sq_z.at[z], sq_z.at[z], za_ss.at[SQ, d], za_rs.at[SQ, d], line[d])
        for d in range(Z - 1)
    ]
    for u, copies in zip(proj, proj_gather):
        finish(u, copies)
    for copy in sq_copies:
        copy.wait_recv()
    squares = jnp.sum(jnp.sum(sq_z[...], axis=0), axis=0, keepdims=True)
    res_out[...] = jnp.sqrt(squares / rows_total)
    for copy in sends:
        copy.wait_send()
    put_ritz.wait()
    put_rimg.wait()


def fused_body(basis, blocks, neighbours, counts, rotation, ritz_values):
    R, Z = lax.axis_size("rows"), lax.axis_size("cols")
    nb, nnb, bs, _ = blocks.shape
    rows, k = basis.shape
    m = rotation.shape[1]
    Q, chunk, piece, wide = R // 2, k // R, k // R // Z, k // PARTS
    vmem = pltpu.VMEM
    dma = pltpu.SemaphoreType.DMA
    any_spec = pl.BlockSpec(memory_space=pl.ANY)
    smem_spec = pl.BlockSpec(memory_space=pltpu.SMEM)
    vmem_spec = pl.BlockSpec(memory_space=pltpu.VMEM)
    pair, sums, res = pl.pallas_call(
        functools.partial(kernel, (nb, nnb, bs, k, m, R, Z)),
        out_shape=(
            jax.ShapeDtypeStruct((2, rows, m), BF16),
            jax.ShapeDtypeStruct((2, chunk, k), F32),
            jax.ShapeDtypeStruct((1, m), F32),
        ),
        in_specs=[smem_spec, smem_spec, any_spec, any_spec, any_spec, any_spec],
        out_specs=(any_spec, vmem_spec, vmem_spec),
        scratch_shapes=[
            vmem((k, m), BF16),
            vmem((1, m), F32),
            vmem((rows, k), BF16),
            vmem((nb, nnb, bs, bs), BF16),
            vmem((rows, nb * bs), BF16),
            vmem((rows, 2 * bs), BF16),
            vmem((2 * bs, k), BF16),
            vmem((rows, k), F32),
            vmem((rows, k), BF16),
            vmem((2, k // 2, rows), BF16),
            vmem((rows, m), F32),
            vmem((rows, m), BF16),
            vmem((rows, m), BF16),
            vmem((SQ, k // 2, wide), F32),
            vmem((SQ, k // 2, wide), BF16),
            vmem((SQ, k // 2, wide), BF16),
            vmem((SQ, chunk, wide), F32),
            vmem((SQ, Q, chunk, wide), BF16),
            vmem((SQ, Q - 1, chunk, wide), BF16),
            vmem((SQ, Z, piece, wide), BF16),
            vmem((SQ, Z - 1, piece, wide), BF16),
            vmem((SQ, Z, piece, wide), BF16),
            vmem((8, m), F32),
            vmem((8, m), F32),
            vmem((Q, 8, m), F32),
            vmem((Z, 8, m), F32),
            dma((6,)),
            dma((2,)),
            dma((2,)),
            dma((SQ + 1,)),
            dma((SQ + 1,)),
            dma((SQ + 1, Q - 1)),
            dma((SQ + 1, Q - 1)),
            dma((SQ, Z - 1)),
            dma((SQ, Z - 1)),
            dma((SQ + 1, Z - 1)),
            dma((SQ + 1, Z - 1)),
        ],
        compiler_params=pltpu.CompilerParams(
            collective_id=0, has_side_effects=True, vmem_limit_bytes=62 * 1024 * 1024
        ),
        name="davidson_step",
    )(neighbours, counts, basis, blocks, rotation, ritz_values.reshape(1, m))
    return pair[0], pair[1], sums[0], sums[1], res.reshape(m)


def body(basis, blocks, neighbours, counts, rotation, ritz_values):
    R, Z = lax.axis_size("rows"), lax.axis_size("cols")
    k = basis.shape[1]
    even = R % 4 == 0 and Z > 1 and k % (16 * R * Z) == 0 and (2 * k // R) % 128 == 0
    chosen = fused_body if even else general_body
    return chosen(basis, blocks, neighbours, counts, rotation, ritz_values)


def solution(mesh):
    return jax.shard_map(
        body,
        mesh=mesh,
        in_specs=(
            P(("rows", "cols"), None),
            P(("rows", "cols"), None, None, None),
            P(("rows", "cols"), None),
            P(("rows", "cols")),
            P(),
            P(),
        ),
        out_specs=(
            P(("rows", "cols"), None),
            P(("rows", "cols"), None),
            P("rows", None),
            P("rows", None),
            P(),
        ),
        check_vma=False,
    )
```

```python
import functools

import jax
import jax.numpy as jnp
from jax import lax
from jax.experimental import pallas as pl
from jax.experimental.pallas import tpu as pltpu
from jax.sharding import PartitionSpec as P


def extended(block, sides, width):
    for axis, dim in sides:
        count = lax.axis_size(axis)
        forward = [(i, i + 1) for i in range(count - 1)]
        backward = [(target, source) for source, target in forward]
        low = lax.ppermute(
            lax.slice_in_dim(block, block.shape[dim] - width, None, axis=dim), axis, forward
        )
        high = lax.ppermute(lax.slice_in_dim(block, 0, width, axis=dim), axis, backward)
        block = jnp.concatenate([low, block, high], axis=dim)
    return block


def general_body(basis, blocks, neighbours, counts, rotation, ritz_values):
    count_blocks = blocks.shape[0]
    slots = blocks.shape[1]
    size_block = blocks.shape[2]
    width = basis.shape[1]
    devices = lax.axis_size("rows") * lax.axis_size("cols")
    rows_total = basis.shape[0] * devices
    first = lax.axis_index(("rows", "cols")) * count_blocks - 1
    local_index = neighbours - first
    live = jnp.arange(slots, dtype=jnp.int32)[None, :] < counts[:, None]
    masked = jnp.where(live[:, :, None, None], blocks, jnp.zeros_like(blocks))
    total = jnp.zeros((count_blocks, size_block, width), jnp.float32)
    own = basis.reshape(count_blocks, size_block, width)
    inside = (local_index >= 1) & (local_index <= count_blocks)
    for slot in range(slots):
        picked = own[jnp.clip(local_index[:, slot] - 1, 0, count_blocks - 1)]
        held = jnp.where(
            inside[:, slot][:, None, None], masked[:, slot], jnp.zeros_like(masked[:, slot])
        )
        total = total + jnp.einsum("brs,bsk->brk", held, picked, preferred_element_type=jnp.float32)
    padded = extended(basis, ((("rows", "cols"), 0),), size_block)
    lower_rows = padded[:size_block]
    upper_rows = padded[-size_block:]
    zero_block = jnp.zeros_like(masked)
    below = jnp.sum(jnp.where((local_index == 0)[:, :, None, None], masked, zero_block), axis=1)
    above = jnp.sum(
        jnp.where((local_index == count_blocks + 1)[:, :, None, None], masked, zero_block), axis=1
    )
    total = total + jnp.einsum("brs,sk->brk", below, lower_rows, preferred_element_type=jnp.float32)
    total = total + jnp.einsum("brs,sk->brk", above, upper_rows, preferred_element_type=jnp.float32)
    image = total.reshape(basis.shape[0], width).astype(jnp.bfloat16)
    joined = jnp.concatenate([basis, image], axis=1)
    partial_rows = lax.psum_scatter(
        jnp.dot(basis.T, joined, preferred_element_type=jnp.float32) / rows_total,
        "rows",
        scatter_dimension=0,
        tiled=True,
    )
    both = lax.psum(partial_rows.astype(jnp.bfloat16), "cols").astype(jnp.float32)
    gram = both[:, :width]
    projected = both[:, width:]
    ritz_full = jnp.dot(basis, rotation, preferred_element_type=jnp.float32)
    image_full = jnp.dot(image, rotation, preferred_element_type=jnp.float32)
    resid = image_full - ritz_values[None, :] * ritz_full
    squares = lax.psum(jnp.sum(resid * resid, axis=0), ("rows", "cols"))
    res_norm = jnp.sqrt(squares / rows_total)
    return (
        ritz_full.astype(jnp.bfloat16),
        image_full.astype(jnp.bfloat16),
        gram,
        projected,
        res_norm,
    )


BF16, F32 = jnp.bfloat16, jnp.float32
PARTS = 2
SQ = 2 * PARTS


def dot(a, b):
    return jnp.dot(a, b, preferred_element_type=F32)


def fold(x):
    return jnp.sum(x.reshape(x.shape[0] // 8, 8, x.shape[1]), axis=0)


def kernel(
    sizes, nbr, cnt, basis_hbm, blocks_hbm, rot_hbm, vals_hbm,
    ritz_hbm, rimg_hbm, sums_out, res_out,
    rot, vals,
    own, blk, mat_in, mat_halo, halo, acc, image, bt, rfull, ritz_v, rimg_v,
    reach, ready, half, core_send, core_recv, part, plane_send, plane_recv,
    z_send, z_recv, gat, sq_own, sq_core, sq_plane, sq_z,
    local_sem, halo_ss, halo_rs, core_ss, core_rs, plane_ss, plane_rs,
    zs_ss, zs_rs, za_ss, za_rs,
):
    nb, nnb, bs, k, m, R, Z = sizes
    Q = R // 2
    rows = nb * bs
    chunk = k // R
    piece = chunk // Z
    rows_total = rows * R * Z
    r = lax.axis_index("rows")
    z = lax.axis_index("cols")
    c = lax.rem(r, 2)
    q = r // 2
    me = r * Z + z
    first = me * nb - 1

    def at(index):
        return (index // Z, lax.rem(index, Z))

    ahead = at(lax.rem(me + 1, R * Z))
    behind = at(lax.rem(me + R * Z - 1, R * Z))
    mate = (q * 2 + 1 - c, z)
    plane_q = [lax.rem(q + d, Q) for d in range(1, Q)]
    plane = [(p * 2 + c, z) for p in plane_q]
    line_z = [lax.rem(z + d, Z) for d in range(1, Z)]
    line = [(r, p) for p in line_z]

    get_basis = pltpu.make_async_copy(basis_hbm, own, local_sem.at[0])
    get_basis.start()
    get_blocks = pltpu.make_async_copy(blocks_hbm, blk, local_sem.at[1])
    get_blocks.start()
    get_rot = pltpu.make_async_copy(rot_hbm, rot, local_sem.at[4])
    get_rot.start()
    get_vals = pltpu.make_async_copy(vals_hbm, vals, local_sem.at[5])
    get_vals.start()

    barrier = pltpu.get_barrier_semaphore()
    peers = [ahead, behind, mate] + plane + line
    for peer in peers:
        pl.semaphore_signal(barrier, inc=1, device_id=peer, device_id_type=pl.DeviceIdType.MESH)
    pl.semaphore_wait(barrier, len(peers))

    sends = []

    def remote(src, dst, ss, rs, to):
        copy = pltpu.make_async_remote_copy(
            src_ref=src, dst_ref=dst, send_sem=ss, recv_sem=rs,
            device_id=to, device_id_type=pl.DeviceIdType.MESH,
        )
        copy.start()
        sends.append(copy)
        return copy

    halo_copies = [
        remote(basis_hbm.at[pl.ds(rows - bs, bs)], halo.at[pl.ds(0, bs)],
               halo_ss.at[0], halo_rs.at[0], ahead),
        remote(basis_hbm.at[pl.ds(0, bs)], halo.at[pl.ds(bs, bs)],
               halo_ss.at[1], halo_rs.at[1], behind),
    ]

    get_basis.wait()
    for i in range(Q):
        turned = own[:, i * 2 * chunk:(i + 1) * 2 * chunk].T
        for side in range(2):
            bt[side, pl.ds(i * chunk, chunk), :] = turned[side * chunk:(side + 1) * chunk]

    wide = k // PARTS

    def columns(which):
        return pl.ds((which % PARTS) * wide, wide)

    def core_phase(which, values):
        core_send[which] = values.astype(BF16)
        return remote(core_send.at[which], core_recv.at[which], core_ss.at[which],
                      core_rs.at[which], mate)

    def plane_phase(which, core_copy):
        core_copy.wait_recv()
        total = half[which] + core_recv[which].astype(F32)
        half[which] = total
        plane_send[which] = total.astype(BF16).reshape(Q, chunk, wide)
        return [
            remote(plane_send.at[which, plane_q[d]], plane_recv.at[which, d],
                   plane_ss.at[which, d], plane_rs.at[which, d], plane[d])
            for d in range(Q - 1)
        ]

    def line_phase(which, copies):
        total = half[which, pl.ds(pl.multiple_of(q * chunk, chunk), chunk), :]
        for d, copy in enumerate(copies):
            copy.wait_recv()
            total = total + plane_recv[which, d].astype(F32)
        part[which] = total
        z_send[which] = total.astype(BF16).reshape(Z, piece, wide)
        return [
            remote(z_send.at[which, line_z[d]], z_recv.at[which, d],
                   zs_ss.at[which, d], zs_rs.at[which, d], line[d])
            for d in range(Z - 1)
        ]

    def gather_phase(which, copies):
        total = part[which, pl.ds(pl.multiple_of(z * piece, piece), piece), :]
        for d, copy in enumerate(copies):
            copy.wait_recv()
            total = total + z_recv[which, d].astype(F32)
        gat[which, z] = total.astype(BF16)
        return [
            remote(gat.at[which, z], gat.at[which, z],
                   za_ss.at[which, d], za_rs.at[which, d], line[d])
            for d in range(Z - 1)
        ]

    def finish(which, copies):
        for copy in copies:
            copy.wait_recv()
        sums_out[which // PARTS, :, columns(which)] = (
            gat[which].astype(F32).reshape(chunk, wide) / rows_total
        )

    gram = range(PARTS)
    proj = range(PARTS, 2 * PARTS)

    gram_core = [core_phase(u, dot(bt[1 - c], own[:, columns(u)])) for u in gram]
    for u in gram:
        half[u] = dot(bt[c], own[:, columns(u)])

    get_rot.wait()
    rfull[...] = dot(own[...], rot[...])
    ritz_v[...] = rfull[...].astype(BF16)
    put_ritz = pltpu.make_async_copy(ritz_v, ritz_hbm, local_sem.at[2])
    put_ritz.start()

    get_blocks.wait()

    @pl.loop(0, nb)
    def _(b):
        n = cnt[b]
        spot = [jnp.where(j < n, nbr[b, j] - first, -1) for j in range(nnb)]
        tiles = [blk[b, j] for j in range(nnb)]
        there = pl.ds(pl.multiple_of(b * bs, bs), bs)
        for s in range(nb + 2):
            total = jnp.zeros((bs, bs), BF16)
            for j in range(nnb):
                weight = jnp.where(spot[j] == s, 1.0, 0.0).astype(F32)
                total = total + tiles[j] * jnp.full((bs, bs), weight, F32).astype(BF16)
            if s == 0:
                mat_halo[there, 0:bs] = total
            elif s == nb + 1:
                mat_halo[there, bs:2 * bs] = total
            else:
                mat_in[there, (s - 1) * bs:s * bs] = total

    gram_plane = [plane_phase(u, gram_core[u]) for u in gram]

    step = min(rows, 2 * bs)

    @pl.loop(0, rows // step)
    def _(i):
        there = pl.ds(pl.multiple_of(i * step, step), step)
        inside = dot(mat_in[there, :], own[...])
        acc[there, :] = inside
        image[there, :] = inside.astype(BF16)

    for side in range(2):
        reach[side] = dot(bt[side], mat_halo[...]).astype(BF16)
    for u in proj:
        ready[u - PARTS] = dot(bt[1 - c], image[:, columns(u)])
    for u in proj:
        half[u] = dot(bt[c], image[:, columns(u)])

    for copy in halo_copies:
        copy.wait_recv()

    proj_core = [
        core_phase(u, ready[u - PARTS] + dot(reach[1 - c], halo[:, columns(u)])) for u in proj
    ]
    for u in proj:
        half[u] += dot(reach[c], halo[:, columns(u)])
    gram_line = [line_phase(u, gram_plane[u]) for u in gram]
    proj_plane = [plane_phase(u, copy) for u, copy in zip(proj, proj_core)]
    get_vals.wait()

    sq_own[...] = jnp.zeros_like(sq_own)

    @pl.loop(0, rows // step)
    def _(i):
        there = pl.ds(pl.multiple_of(i * step, step), step)
        outside = dot(mat_halo[there, :], halo[...])
        full = dot((acc[there, :] + outside).astype(BF16), rot[...])
        rimg_v[there, :] = full.astype(BF16)
        resid = full - vals[...] * rfull[there, :]
        sq_own[...] += fold(resid * resid)

    put_rimg = pltpu.make_async_copy(rimg_v, rimg_hbm, local_sem.at[3])
    put_rimg.start()
    sq_copy = remote(sq_own, sq_core, core_ss.at[SQ], core_rs.at[SQ], mate)

    gram_gather = [gather_phase(u, gram_line[u]) for u in gram]
    proj_line = [line_phase(u, copies) for u, copies in zip(proj, proj_plane)]
    sq_copy.wait_recv()
    sq_plane[q] = sq_own[...] + sq_core[...]
    sq_copies = [
        remote(sq_plane.at[q], sq_plane.at[q], plane_ss.at[SQ, d], plane_rs.at[SQ, d], plane[d])
        for d in range(Q - 1)
    ]
    for u in gram:
        finish(u, gram_gather[u])
    proj_gather = [gather_phase(u, copies) for u, copies in zip(proj, proj_line)]
    for copy in sq_copies:
        copy.wait_recv()
    sq_z[z] = jnp.sum(sq_plane[...], axis=0)
    sq_copies = [
        remote(sq_z.at[z], sq_z.at[z], za_ss.at[SQ, d], za_rs.at[SQ, d], line[d])
        for d in range(Z - 1)
    ]
    for u, copies in zip(proj, proj_gather):
        finish(u, copies)
    for copy in sq_copies:
        copy.wait_recv()
    squares = jnp.sum(jnp.sum(sq_z[...], axis=0), axis=0, keepdims=True)
    res_out[...] = jnp.sqrt(squares / rows_total)
    for copy in sends:
        copy.wait_send()
    put_ritz.wait()
    put_rimg.wait()


def fused_body(basis, blocks, neighbours, counts, rotation, ritz_values):
    R, Z = lax.axis_size("rows"), lax.axis_size("cols")
    nb, nnb, bs, _ = blocks.shape
    rows, k = basis.shape
    m = rotation.shape[1]
    Q, chunk, piece, wide = R // 2, k // R, k // R // Z, k // PARTS
    vmem = pltpu.VMEM
    dma = pltpu.SemaphoreType.DMA
    any_spec = pl.BlockSpec(memory_space=pl.ANY)
    smem_spec = pl.BlockSpec(memory_space=pltpu.SMEM)
    vmem_spec = pl.BlockSpec(memory_space=pltpu.VMEM)
    ritz, rimg, sums, res = pl.pallas_call(
        functools.partial(kernel, (nb, nnb, bs, k, m, R, Z)),
        out_shape=(
            jax.ShapeDtypeStruct((rows, m), BF16),
            jax.ShapeDtypeStruct((rows, m), BF16),
            jax.ShapeDtypeStruct((2, chunk, k), F32),
            jax.ShapeDtypeStruct((1, m), F32),
        ),
        in_specs=[smem_spec, smem_spec, any_spec, any_spec, any_spec, any_spec],
        out_specs=(any_spec, any_spec, vmem_spec, vmem_spec),
        scratch_shapes=[
            vmem((k, m), BF16),
            vmem((1, m), F32),
            vmem((rows, k), BF16),
            vmem((nb, nnb, bs, bs), BF16),
            vmem((rows, nb * bs), BF16),
            vmem((rows, 2 * bs), BF16),
            vmem((2 * bs, k), BF16),
            vmem((rows, k), F32),
            vmem((rows, k), BF16),
            vmem((2, k // 2, rows), BF16),
            vmem((rows, m), F32),
            vmem((rows, m), BF16),
            vmem((rows, m), BF16),
            vmem((2, k // 2, 2 * bs), BF16),
            vmem((PARTS, k // 2, wide), F32),
            vmem((SQ, k // 2, wide), F32),
            vmem((SQ, k // 2, wide), BF16),
            vmem((SQ, k // 2, wide), BF16),
            vmem((SQ, chunk, wide), F32),
            vmem((SQ, Q, chunk, wide), BF16),
            vmem((SQ, Q - 1, chunk, wide), BF16),
            vmem((SQ, Z, piece, wide), BF16),
            vmem((SQ, Z - 1, piece, wide), BF16),
            vmem((SQ, Z, piece, wide), BF16),
            vmem((8, m), F32),
            vmem((8, m), F32),
            vmem((Q, 8, m), F32),
            vmem((Z, 8, m), F32),
            dma((6,)),
            dma((2,)),
            dma((2,)),
            dma((SQ + 1,)),
            dma((SQ + 1,)),
            dma((SQ + 1, Q - 1)),
            dma((SQ + 1, Q - 1)),
            dma((SQ, Z - 1)),
            dma((SQ, Z - 1)),
            dma((SQ + 1, Z - 1)),
            dma((SQ + 1, Z - 1)),
        ],
        compiler_params=pltpu.CompilerParams(
            collective_id=0, has_side_effects=True, vmem_limit_bytes=62 * 1024 * 1024
        ),
        name="davidson_step",
    )(neighbours, counts, basis, blocks, rotation, ritz_values.reshape(1, m))
    return ritz, rimg, sums[0], sums[1], res.reshape(m)


def body(basis, blocks, neighbours, counts, rotation, ritz_values):
    R, Z = lax.axis_size("rows"), lax.axis_size("cols")
    k = basis.shape[1]
    even = R % 4 == 0 and Z > 1 and k % (16 * R * Z) == 0 and (2 * k // R) % 128 == 0
    chosen = fused_body if even else general_body
    return chosen(basis, blocks, neighbours, counts, rotation, ritz_values)


def solution(mesh):
    return jax.shard_map(
        body,
        mesh=mesh,
        in_specs=(
            P(("rows", "cols"), None),
            P(("rows", "cols"), None, None, None),
            P(("rows", "cols"), None),
            P(("rows", "cols")),
            P(),
            P(),
        ),
        out_specs=(
            P(("rows", "cols"), None),
            P(("rows", "cols"), None),
            P("rows", None),
            P("rows", None),
            P(),
        ),
        check_vma=False,
    )
```

```python
import functools

import jax
import jax.numpy as jnp
from jax import lax
from jax.experimental import pallas as pl
from jax.experimental.pallas import tpu as pltpu
from jax.sharding import PartitionSpec as P


def extended(block, sides, width):
    for axis, dim in sides:
        count = lax.axis_size(axis)
        forward = [(i, i + 1) for i in range(count - 1)]
        backward = [(target, source) for source, target in forward]
        low = lax.ppermute(
            lax.slice_in_dim(block, block.shape[dim] - width, None, axis=dim), axis, forward
        )
        high = lax.ppermute(lax.slice_in_dim(block, 0, width, axis=dim), axis, backward)
        block = jnp.concatenate([low, block, high], axis=dim)
    return block


def general_body(basis, blocks, neighbours, counts, rotation, ritz_values):
    count_blocks = blocks.shape[0]
    slots = blocks.shape[1]
    size_block = blocks.shape[2]
    width = basis.shape[1]
    devices = lax.axis_size("rows") * lax.axis_size("cols")
    rows_total = basis.shape[0] * devices
    first = lax.axis_index(("rows", "cols")) * count_blocks - 1
    local_index = neighbours - first
    live = jnp.arange(slots, dtype=jnp.int32)[None, :] < counts[:, None]
    masked = jnp.where(live[:, :, None, None], blocks, jnp.zeros_like(blocks))
    total = jnp.zeros((count_blocks, size_block, width), jnp.float32)
    own = basis.reshape(count_blocks, size_block, width)
    inside = (local_index >= 1) & (local_index <= count_blocks)
    for slot in range(slots):
        picked = own[jnp.clip(local_index[:, slot] - 1, 0, count_blocks - 1)]
        held = jnp.where(
            inside[:, slot][:, None, None], masked[:, slot], jnp.zeros_like(masked[:, slot])
        )
        total = total + jnp.einsum("brs,bsk->brk", held, picked, preferred_element_type=jnp.float32)
    padded = extended(basis, ((("rows", "cols"), 0),), size_block)
    lower_rows = padded[:size_block]
    upper_rows = padded[-size_block:]
    zero_block = jnp.zeros_like(masked)
    below = jnp.sum(jnp.where((local_index == 0)[:, :, None, None], masked, zero_block), axis=1)
    above = jnp.sum(
        jnp.where((local_index == count_blocks + 1)[:, :, None, None], masked, zero_block), axis=1
    )
    total = total + jnp.einsum("brs,sk->brk", below, lower_rows, preferred_element_type=jnp.float32)
    total = total + jnp.einsum("brs,sk->brk", above, upper_rows, preferred_element_type=jnp.float32)
    image = total.reshape(basis.shape[0], width).astype(jnp.bfloat16)
    joined = jnp.concatenate([basis, image], axis=1)
    partial_rows = lax.psum_scatter(
        jnp.dot(basis.T, joined, preferred_element_type=jnp.float32) / rows_total,
        "rows",
        scatter_dimension=0,
        tiled=True,
    )
    both = lax.psum(partial_rows.astype(jnp.bfloat16), "cols").astype(jnp.float32)
    gram = both[:, :width]
    projected = both[:, width:]
    ritz_full = jnp.dot(basis, rotation, preferred_element_type=jnp.float32)
    image_full = jnp.dot(image, rotation, preferred_element_type=jnp.float32)
    resid = image_full - ritz_values[None, :] * ritz_full
    squares = lax.psum(jnp.sum(resid * resid, axis=0), ("rows", "cols"))
    res_norm = jnp.sqrt(squares / rows_total)
    return (
        ritz_full.astype(jnp.bfloat16),
        image_full.astype(jnp.bfloat16),
        gram,
        projected,
        res_norm,
    )


BF16, F32 = jnp.bfloat16, jnp.float32
PARTS = 2
SQ = 2 * PARTS


def dot(a, b):
    return jnp.dot(a, b, preferred_element_type=F32)


def fold(x):
    return jnp.sum(x.reshape(x.shape[0] // 8, 8, x.shape[1]), axis=0)


def kernel(
    sizes, nbr_hbm, cnt_hbm, basis_hbm, blocks_hbm, rot_hbm, vals_hbm,
    ritz_v, rimg_v, sums_out, res_out,
    nbr, cnt, rot, vals,
    own, blk, mat_in, mat_halo, halo, acc, image, bt, rfull,
    reach, ready, half, core_send, core_recv, part, plane_send, plane_recv,
    z_send, z_recv, gat, sq_own, sq_core, sq_plane, sq_z,
    local_sem, halo_ss, halo_rs, core_ss, core_rs, plane_ss, plane_rs,
    zs_ss, zs_rs, za_ss, za_rs,
):
    nb, nnb, bs, k, m, R, Z = sizes
    Q = R // 2
    rows = nb * bs
    chunk = k // R
    piece = chunk // Z
    rows_total = rows * R * Z
    r = lax.axis_index("rows")
    z = lax.axis_index("cols")
    c = lax.rem(r, 2)
    q = r // 2
    me = r * Z + z
    first = me * nb - 1

    def at(index):
        return (index // Z, lax.rem(index, Z))

    ahead = at(lax.rem(me + 1, R * Z))
    behind = at(lax.rem(me + R * Z - 1, R * Z))
    mate = (q * 2 + 1 - c, z)
    plane_q = [lax.rem(q + d, Q) for d in range(1, Q)]
    plane = [(p * 2 + c, z) for p in plane_q]
    line_z = [lax.rem(z + d, Z) for d in range(1, Z)]
    line = [(r, p) for p in line_z]

    get_basis = pltpu.make_async_copy(basis_hbm, own, local_sem.at[0])
    get_basis.start()
    get_blocks = pltpu.make_async_copy(blocks_hbm, blk, local_sem.at[1])
    get_blocks.start()
    get_nbr = pltpu.make_async_copy(nbr_hbm, nbr, local_sem.at[2])
    get_nbr.start()
    get_cnt = pltpu.make_async_copy(cnt_hbm, cnt, local_sem.at[3])
    get_cnt.start()
    get_rot = pltpu.make_async_copy(rot_hbm, rot, local_sem.at[4])
    get_rot.start()
    get_vals = pltpu.make_async_copy(vals_hbm, vals, local_sem.at[5])
    get_vals.start()

    barrier = pltpu.get_barrier_semaphore()
    peers = [ahead, behind, mate] + plane + line
    for peer in peers:
        pl.semaphore_signal(barrier, inc=1, device_id=peer, device_id_type=pl.DeviceIdType.MESH)
    pl.semaphore_wait(barrier, len(peers))

    sends = []

    def remote(src, dst, ss, rs, to):
        copy = pltpu.make_async_remote_copy(
            src_ref=src, dst_ref=dst, send_sem=ss, recv_sem=rs,
            device_id=to, device_id_type=pl.DeviceIdType.MESH,
        )
        copy.start()
        sends.append(copy)
        return copy

    halo_copies = [
        remote(basis_hbm.at[pl.ds(rows - bs, bs)], halo.at[pl.ds(0, bs)],
               halo_ss.at[0], halo_rs.at[0], ahead),
        remote(basis_hbm.at[pl.ds(0, bs)], halo.at[pl.ds(bs, bs)],
               halo_ss.at[1], halo_rs.at[1], behind),
    ]

    get_basis.wait()
    for i in range(Q):
        turned = own[:, i * 2 * chunk:(i + 1) * 2 * chunk].T
        for side in range(2):
            bt[side, pl.ds(i * chunk, chunk), :] = turned[side * chunk:(side + 1) * chunk]

    wide = k // PARTS

    def columns(which):
        return pl.ds((which % PARTS) * wide, wide)

    def core_phase(which, values):
        core_send[which] = values.astype(BF16)
        return remote(core_send.at[which], core_recv.at[which], core_ss.at[which],
                      core_rs.at[which], mate)

    def plane_phase(which, core_copy):
        core_copy.wait_recv()
        total = half[which] + core_recv[which].astype(F32)
        half[which] = total
        plane_send[which] = total.astype(BF16).reshape(Q, chunk, wide)
        return [
            remote(plane_send.at[which, plane_q[d]], plane_recv.at[which, d],
                   plane_ss.at[which, d], plane_rs.at[which, d], plane[d])
            for d in range(Q - 1)
        ]

    def line_phase(which, copies):
        total = half[which, pl.ds(pl.multiple_of(q * chunk, chunk), chunk), :]
        for d, copy in enumerate(copies):
            copy.wait_recv()
            total = total + plane_recv[which, d].astype(F32)
        part[which] = total
        z_send[which] = total.astype(BF16).reshape(Z, piece, wide)
        return [
            remote(z_send.at[which, line_z[d]], z_recv.at[which, d],
                   zs_ss.at[which, d], zs_rs.at[which, d], line[d])
            for d in range(Z - 1)
        ]

    def gather_phase(which, copies):
        total = part[which, pl.ds(pl.multiple_of(z * piece, piece), piece), :]
        for d, copy in enumerate(copies):
            copy.wait_recv()
            total = total + z_recv[which, d].astype(F32)
        gat[which, z] = total.astype(BF16)
        return [
            remote(gat.at[which, z], gat.at[which, z],
                   za_ss.at[which, d], za_rs.at[which, d], line[d])
            for d in range(Z - 1)
        ]

    def finish(which, copies):
        for copy in copies:
            copy.wait_recv()
        sums_out[which // PARTS, :, columns(which)] = (
            gat[which].astype(F32).reshape(chunk, wide) / rows_total
        )

    gram = range(PARTS)
    proj = range(PARTS, 2 * PARTS)

    gram_core = [core_phase(u, dot(bt[1 - c], own[:, columns(u)])) for u in gram]
    for u in gram:
        half[u] = dot(bt[c], own[:, columns(u)])

    get_rot.wait()
    rfull[...] = dot(own[...], rot[...])
    ritz_v[...] = rfull[...].astype(BF16)

    get_blocks.wait()
    get_nbr.wait()
    get_cnt.wait()

    @pl.loop(0, nb)
    def _(b):
        n = cnt[0, b]
        spot = [jnp.where(j < n, nbr[b, j] - first, -1) for j in range(nnb)]
        tiles = [blk[b, j] for j in range(nnb)]
        there = pl.ds(pl.multiple_of(b * bs, bs), bs)
        for s in range(nb + 2):
            total = jnp.zeros((bs, bs), BF16)
            for j in range(nnb):
                weight = jnp.where(spot[j] == s, 1.0, 0.0).astype(F32)
                total = total + tiles[j] * jnp.full((bs, bs), weight, F32).astype(BF16)
            if s == 0:
                mat_halo[there, 0:bs] = total
            elif s == nb + 1:
                mat_halo[there, bs:2 * bs] = total
            else:
                mat_in[there, (s - 1) * bs:s * bs] = total

    gram_plane = [plane_phase(u, gram_core[u]) for u in gram]

    step = min(rows, 2 * bs)

    @pl.loop(0, rows // step)
    def _(i):
        there = pl.ds(pl.multiple_of(i * step, step), step)
        inside = dot(mat_in[there, :], own[...])
        acc[there, :] = inside
        image[there, :] = inside.astype(BF16)

    for side in range(2):
        reach[side] = dot(bt[side], mat_halo[...]).astype(BF16)
    for u in proj:
        ready[u - PARTS] = dot(bt[1 - c], image[:, columns(u)])
    for u in proj:
        half[u] = dot(bt[c], image[:, columns(u)])

    for copy in halo_copies:
        copy.wait_recv()

    proj_core = [
        core_phase(u, ready[u - PARTS] + dot(reach[1 - c], halo[:, columns(u)])) for u in proj
    ]
    for u in proj:
        half[u] += dot(reach[c], halo[:, columns(u)])
    gram_line = [line_phase(u, gram_plane[u]) for u in gram]
    proj_plane = [plane_phase(u, copy) for u, copy in zip(proj, proj_core)]
    get_vals.wait()

    sq_own[...] = jnp.zeros_like(sq_own)

    @pl.loop(0, rows // step)
    def _(i):
        there = pl.ds(pl.multiple_of(i * step, step), step)
        outside = dot(mat_halo[there, :], halo[...])
        full = dot((acc[there, :] + outside).astype(BF16), rot[...])
        rimg_v[there, :] = full.astype(BF16)
        resid = full - vals[...] * rfull[there, :]
        sq_own[...] += fold(resid * resid)

    sq_copy = remote(sq_own, sq_core, core_ss.at[SQ], core_rs.at[SQ], mate)

    gram_gather = [gather_phase(u, gram_line[u]) for u in gram]
    proj_line = [line_phase(u, copies) for u, copies in zip(proj, proj_plane)]
    sq_copy.wait_recv()
    sq_plane[q] = sq_own[...] + sq_core[...]
    sq_copies = [
        remote(sq_plane.at[q], sq_plane.at[q], plane_ss.at[SQ, d], plane_rs.at[SQ, d], plane[d])
        for d in range(Q - 1)
    ]
    for u in gram:
        finish(u, gram_gather[u])
    proj_gather = [gather_phase(u, copies) for u, copies in zip(proj, proj_line)]
    for copy in sq_copies:
        copy.wait_recv()
    sq_z[z] = jnp.sum(sq_plane[...], axis=0)
    sq_copies = [
        remote(sq_z.at[z], sq_z.at[z], za_ss.at[SQ, d], za_rs.at[SQ, d], line[d])
        for d in range(Z - 1)
    ]
    for u, copies in zip(proj, proj_gather):
        finish(u, copies)
    for copy in sq_copies:
        copy.wait_recv()
    squares = jnp.sum(jnp.sum(sq_z[...], axis=0), axis=0, keepdims=True)
    res_out[...] = jnp.sqrt(squares / rows_total)
    for copy in sends:
        copy.wait_send()


def fused_body(basis, blocks, neighbours, counts, rotation, ritz_values):
    R, Z = lax.axis_size("rows"), lax.axis_size("cols")
    nb, nnb, bs, _ = blocks.shape
    rows, k = basis.shape
    m = rotation.shape[1]
    Q, chunk, piece, wide = R // 2, k // R, k // R // Z, k // PARTS
    vmem = pltpu.VMEM
    dma = pltpu.SemaphoreType.DMA
    hbm_spec = pl.BlockSpec(memory_space=pltpu.HBM)
    vmem_spec = pl.BlockSpec(memory_space=pltpu.VMEM)
    ritz, rimg, sums, res = pl.pallas_call(
        functools.partial(kernel, (nb, nnb, bs, k, m, R, Z)),
        out_shape=(
            jax.ShapeDtypeStruct((rows, m), BF16),
            jax.ShapeDtypeStruct((rows, m), BF16),
            jax.ShapeDtypeStruct((2, chunk, k), F32),
            jax.ShapeDtypeStruct((1, m), F32),
        ),
        in_specs=[hbm_spec] * 6,
        out_specs=(vmem_spec,) * 4,
        scratch_shapes=[
            pltpu.SMEM((nb, nnb), jnp.int32),
            pltpu.SMEM((1, nb), jnp.int32),
            vmem((k, m), BF16),
            vmem((1, m), F32),
            vmem((rows, k), BF16),
            vmem((nb, nnb, bs, bs), BF16),
            vmem((rows, nb * bs), BF16),
            vmem((rows, 2 * bs), BF16),
            vmem((2 * bs, k), BF16),
            vmem((rows, k), F32),
            vmem((rows, k), BF16),
            vmem((2, k // 2, rows), BF16),
            vmem((rows, m), F32),
            vmem((2, k // 2, 2 * bs), BF16),
            vmem((PARTS, k // 2, wide), F32),
            vmem((SQ, k // 2, wide), F32),
            vmem((SQ, k // 2, wide), BF16),
            vmem((SQ, k // 2, wide), BF16),
            vmem((SQ, chunk, wide), F32),
            vmem((SQ, Q, chunk, wide), BF16),
            vmem((SQ, Q - 1, chunk, wide), BF16),
            vmem((SQ, Z, piece, wide), BF16),
            vmem((SQ, Z - 1, piece, wide), BF16),
            vmem((SQ, Z, piece, wide), BF16),
            vmem((8, m), F32),
            vmem((8, m), F32),
            vmem((Q, 8, m), F32),
            vmem((Z, 8, m), F32),
            dma((6,)),
            dma((2,)),
            dma((2,)),
            dma((SQ + 1,)),
            dma((SQ + 1,)),
            dma((SQ + 1, Q - 1)),
            dma((SQ + 1, Q - 1)),
            dma((SQ, Z - 1)),
            dma((SQ, Z - 1)),
            dma((SQ + 1, Z - 1)),
            dma((SQ + 1, Z - 1)),
        ],
        compiler_params=pltpu.CompilerParams(
            collective_id=0, has_side_effects=True, vmem_limit_bytes=36 * 1024 * 1024
        ),
        name="davidson_step",
    )(*[
        pltpu.with_memory_space_constraint(x, pltpu.HBM)
        for x in (neighbours, counts.reshape(1, nb), basis, blocks, rotation,
                  ritz_values.reshape(1, m))
    ])
    return ritz, rimg, sums[0], sums[1], res.reshape(m)


def body(basis, blocks, neighbours, counts, rotation, ritz_values):
    R, Z = lax.axis_size("rows"), lax.axis_size("cols")
    k = basis.shape[1]
    even = R % 4 == 0 and Z > 1 and k % (16 * R * Z) == 0 and (2 * k // R) % 128 == 0
    chosen = fused_body if even else general_body
    return chosen(basis, blocks, neighbours, counts, rotation, ritz_values)


def solution(mesh):
    return jax.shard_map(
        body,
        mesh=mesh,
        in_specs=(
            P(("rows", "cols"), None),
            P(("rows", "cols"), None, None, None),
            P(("rows", "cols"), None),
            P(("rows", "cols")),
            P(),
            P(),
        ),
        out_specs=(
            P(("rows", "cols"), None),
            P(("rows", "cols"), None),
            P("rows", None),
            P("rows", None),
            P(),
        ),
        check_vma=False,
    )
```

```python
import functools

import jax
import jax.numpy as jnp
from jax import lax
from jax.experimental import pallas as pl
from jax.experimental.pallas import tpu as pltpu
from jax.sharding import PartitionSpec as P


def extended(block, sides, width):
    for axis, dim in sides:
        count = lax.axis_size(axis)
        forward = [(i, i + 1) for i in range(count - 1)]
        backward = [(target, source) for source, target in forward]
        low = lax.ppermute(
            lax.slice_in_dim(block, block.shape[dim] - width, None, axis=dim), axis, forward
        )
        high = lax.ppermute(lax.slice_in_dim(block, 0, width, axis=dim), axis, backward)
        block = jnp.concatenate([low, block, high], axis=dim)
    return block


def general_body(basis, blocks, neighbours, counts, rotation, ritz_values):
    count_blocks = blocks.shape[0]
    slots = blocks.shape[1]
    size_block = blocks.shape[2]
    width = basis.shape[1]
    devices = lax.axis_size("rows") * lax.axis_size("cols")
    rows_total = basis.shape[0] * devices
    first = lax.axis_index(("rows", "cols")) * count_blocks - 1
    local_index = neighbours - first
    live = jnp.arange(slots, dtype=jnp.int32)[None, :] < counts[:, None]
    masked = jnp.where(live[:, :, None, None], blocks, jnp.zeros_like(blocks))
    total = jnp.zeros((count_blocks, size_block, width), jnp.float32)
    own = basis.reshape(count_blocks, size_block, width)
    inside = (local_index >= 1) & (local_index <= count_blocks)
    for slot in range(slots):
        picked = own[jnp.clip(local_index[:, slot] - 1, 0, count_blocks - 1)]
        held = jnp.where(
            inside[:, slot][:, None, None], masked[:, slot], jnp.zeros_like(masked[:, slot])
        )
        total = total + jnp.einsum("brs,bsk->brk", held, picked, preferred_element_type=jnp.float32)
    padded = extended(basis, ((("rows", "cols"), 0),), size_block)
    lower_rows = padded[:size_block]
    upper_rows = padded[-size_block:]
    zero_block = jnp.zeros_like(masked)
    below = jnp.sum(jnp.where((local_index == 0)[:, :, None, None], masked, zero_block), axis=1)
    above = jnp.sum(
        jnp.where((local_index == count_blocks + 1)[:, :, None, None], masked, zero_block), axis=1
    )
    total = total + jnp.einsum("brs,sk->brk", below, lower_rows, preferred_element_type=jnp.float32)
    total = total + jnp.einsum("brs,sk->brk", above, upper_rows, preferred_element_type=jnp.float32)
    image = total.reshape(basis.shape[0], width).astype(jnp.bfloat16)
    joined = jnp.concatenate([basis, image], axis=1)
    partial_rows = lax.psum_scatter(
        jnp.dot(basis.T, joined, preferred_element_type=jnp.float32) / rows_total,
        "rows",
        scatter_dimension=0,
        tiled=True,
    )
    both = lax.psum(partial_rows.astype(jnp.bfloat16), "cols").astype(jnp.float32)
    gram = both[:, :width]
    projected = both[:, width:]
    ritz_full = jnp.dot(basis, rotation, preferred_element_type=jnp.float32)
    image_full = jnp.dot(image, rotation, preferred_element_type=jnp.float32)
    resid = image_full - ritz_values[None, :] * ritz_full
    squares = lax.psum(jnp.sum(resid * resid, axis=0), ("rows", "cols"))
    res_norm = jnp.sqrt(squares / rows_total)
    return (
        ritz_full.astype(jnp.bfloat16),
        image_full.astype(jnp.bfloat16),
        gram,
        projected,
        res_norm,
    )


BF16, F32 = jnp.bfloat16, jnp.float32
PARTS = 2
SQ = 2 * PARTS


def dot(a, b):
    return jnp.dot(a, b, preferred_element_type=F32)


def fold(x):
    return jnp.sum(x.reshape(x.shape[0] // 8, 8, x.shape[1]), axis=0)


def kernel(
    sizes, nbr_hbm, cnt_hbm, basis_hbm, blocks_hbm, rot_hbm, vals_hbm,
    ritz_v, rimg_v, sums_out, res_out,
    nbr, cnt, rot, vals,
    own, blk, mat_in, mat_halo, halo, acc, image, bt, rfull,
    reach, ready, half, core_send, core_recv, part, plane_send, plane_recv,
    z_send, z_recv, gat, spread, sq_own, sq_core, sq_plane, sq_z,
    local_sem, halo_ss, halo_rs, core_ss, core_rs, plane_ss, plane_rs,
    zs_ss, zs_rs, za_ss, za_rs,
):
    nb, nnb, bs, k, m, R, Z = sizes
    Q = R // 2
    rows = nb * bs
    chunk = k // R
    piece = chunk // Z
    rows_total = rows * R * Z
    r = lax.axis_index("rows")
    z = lax.axis_index("cols")
    c = lax.rem(r, 2)
    q = r // 2
    me = r * Z + z
    first = me * nb - 1

    def at(index):
        return (index // Z, lax.rem(index, Z))

    ahead = at(lax.rem(me + 1, R * Z))
    behind = at(lax.rem(me + R * Z - 1, R * Z))
    mate = (q * 2 + 1 - c, z)
    plane_q = [lax.rem(q + d, Q) for d in range(1, Q)]
    plane = [(p * 2 + c, z) for p in plane_q]
    line_z = [lax.rem(z + d, Z) for d in range(1, Z)]
    line = [(r, p) for p in line_z]

    get_basis = pltpu.make_async_copy(basis_hbm, own, local_sem.at[0])
    get_basis.start()
    get_blocks = pltpu.make_async_copy(blocks_hbm, blk, local_sem.at[1])
    get_blocks.start()
    get_nbr = pltpu.make_async_copy(nbr_hbm, nbr, local_sem.at[2])
    get_nbr.start()
    get_cnt = pltpu.make_async_copy(cnt_hbm, cnt, local_sem.at[3])
    get_cnt.start()
    get_rot = pltpu.make_async_copy(rot_hbm, rot, local_sem.at[4])
    get_rot.start()
    get_vals = pltpu.make_async_copy(vals_hbm, vals, local_sem.at[5])
    get_vals.start()

    barrier = pltpu.get_barrier_semaphore()
    peers = [ahead, behind, mate] + plane + line
    for peer in peers:
        pl.semaphore_signal(barrier, inc=1, device_id=peer, device_id_type=pl.DeviceIdType.MESH)
    pl.semaphore_wait(barrier, len(peers))

    sends = []

    def remote(src, dst, ss, rs, to):
        copy = pltpu.make_async_remote_copy(
            src_ref=src, dst_ref=dst, send_sem=ss, recv_sem=rs,
            device_id=to, device_id_type=pl.DeviceIdType.MESH,
        )
        copy.start()
        sends.append(copy)
        return copy

    halo_copies = [
        remote(basis_hbm.at[pl.ds(rows - bs, bs)], halo.at[pl.ds(0, bs)],
               halo_ss.at[0], halo_rs.at[0], ahead),
        remote(basis_hbm.at[pl.ds(0, bs)], halo.at[pl.ds(bs, bs)],
               halo_ss.at[1], halo_rs.at[1], behind),
    ]

    get_basis.wait()
    for i in range(Q):
        turned = own[:, i * 2 * chunk:(i + 1) * 2 * chunk].T
        for side in range(2):
            bt[side, pl.ds(i * chunk, chunk), :] = turned[side * chunk:(side + 1) * chunk]

    wide = k // PARTS

    def columns(which):
        return pl.ds((which % PARTS) * wide, wide)

    def core_phase(which, values):
        core_send[which] = values.astype(BF16)
        return remote(core_send.at[which], core_recv.at[which], core_ss.at[which],
                      core_rs.at[which], mate)

    def plane_phase(which, core_copy):
        core_copy.wait_recv()
        total = half[which] + core_recv[which].astype(F32)
        half[which] = total
        plane_send[which] = total.astype(BF16).reshape(Q, chunk, wide)
        return [
            remote(plane_send.at[which, plane_q[d]], plane_recv.at[which, d],
                   plane_ss.at[which, d], plane_rs.at[which, d], plane[d])
            for d in range(Q - 1)
        ]

    def line_phase(which, copies):
        total = half[which, pl.ds(pl.multiple_of(q * chunk, chunk), chunk), :]
        for d, copy in enumerate(copies):
            copy.wait_recv()
            total = total + plane_recv[which, d].astype(F32)
        part[which] = total
        z_send[which] = total.astype(BF16).reshape(Z, piece, wide)
        return [
            remote(z_send.at[which, line_z[d]], z_recv.at[which, d],
                   zs_ss.at[which, d], zs_rs.at[which, d], line[d])
            for d in range(Z - 1)
        ]

    def spread_phase(which, copies):
        total = half[which, pl.ds(pl.multiple_of(q * chunk, chunk), chunk), :]
        for d, copy in enumerate(copies):
            copy.wait_recv()
            total = total + plane_recv[which, d].astype(F32)
        u = which - PARTS
        spread[u, z] = total.astype(BF16)
        return [
            remote(spread.at[u, z], spread.at[u, z],
                   zs_ss.at[which, d], zs_rs.at[which, d], line[d])
            for d in range(Z - 1)
        ]

    def gather_phase(which, copies):
        total = part[which, pl.ds(pl.multiple_of(z * piece, piece), piece), :]
        for d, copy in enumerate(copies):
            copy.wait_recv()
            total = total + z_recv[which, d].astype(F32)
        gat[which, z] = total.astype(BF16)
        return [
            remote(gat.at[which, z], gat.at[which, z],
                   za_ss.at[which, d], za_rs.at[which, d], line[d])
            for d in range(Z - 1)
        ]

    def finish(which, copies):
        for copy in copies:
            copy.wait_recv()
        sums_out[which // PARTS, :, columns(which)] = (
            gat[which].astype(F32).reshape(chunk, wide) / rows_total
        )

    gram = range(PARTS)
    proj = range(PARTS, 2 * PARTS)

    gram_core = [core_phase(u, dot(bt[1 - c], own[:, columns(u)])) for u in gram]
    for u in gram:
        half[u] = dot(bt[c], own[:, columns(u)])

    get_rot.wait()
    rfull[...] = dot(own[...], rot[...])
    ritz_v[...] = rfull[...].astype(BF16)

    gram_plane = [plane_phase(u, gram_core[u]) for u in gram]

    get_blocks.wait()
    get_nbr.wait()
    get_cnt.wait()

    @pl.loop(0, nb)
    def _(b):
        n = cnt[0, b]
        spot = [jnp.where(j < n, nbr[b, j] - first, -1) for j in range(nnb)]
        tiles = [blk[b, j] for j in range(nnb)]
        there = pl.ds(pl.multiple_of(b * bs, bs), bs)
        for s in range(nb + 2):
            total = jnp.zeros((bs, bs), BF16)
            for j in range(nnb):
                weight = jnp.where(spot[j] == s, 1.0, 0.0).astype(F32)
                total = total + tiles[j] * jnp.full((bs, bs), weight, F32).astype(BF16)
            if s == 0:
                mat_halo[there, 0:bs] = total
            elif s == nb + 1:
                mat_halo[there, bs:2 * bs] = total
            else:
                mat_in[there, (s - 1) * bs:s * bs] = total


    step = min(rows, 2 * bs)

    @pl.loop(0, rows // step)
    def _(i):
        there = pl.ds(pl.multiple_of(i * step, step), step)
        inside = dot(mat_in[there, :], own[...])
        acc[there, :] = inside
        image[there, :] = inside.astype(BF16)

    for side in range(2):
        reach[side] = dot(bt[side], mat_halo[...]).astype(BF16)
    for u in proj:
        ready[u - PARTS] = dot(bt[1 - c], image[:, columns(u)])
    for u in proj:
        half[u] = dot(bt[c], image[:, columns(u)])

    for copy in halo_copies:
        copy.wait_recv()

    proj_core = [
        core_phase(u, ready[u - PARTS] + dot(reach[1 - c], halo[:, columns(u)])) for u in proj
    ]
    for u in proj:
        half[u] += dot(reach[c], halo[:, columns(u)])
    gram_line = [line_phase(u, gram_plane[u]) for u in gram]
    proj_plane = [plane_phase(u, copy) for u, copy in zip(proj, proj_core)]
    get_vals.wait()

    sq_own[...] = jnp.zeros_like(sq_own)

    @pl.loop(0, rows // step)
    def _(i):
        there = pl.ds(pl.multiple_of(i * step, step), step)
        outside = dot(mat_halo[there, :], halo[...])
        full = dot((acc[there, :] + outside).astype(BF16), rot[...])
        rimg_v[there, :] = full.astype(BF16)
        resid = full - vals[...] * rfull[there, :]
        sq_own[...] += fold(resid * resid)

    sq_copy = remote(sq_own, sq_core, core_ss.at[SQ], core_rs.at[SQ], mate)

    gram_gather = [gather_phase(u, gram_line[u]) for u in gram]
    proj_spread = [spread_phase(u, copies) for u, copies in zip(proj, proj_plane)]
    sq_copy.wait_recv()
    sq_plane[q] = sq_own[...] + sq_core[...]
    sq_copies = [
        remote(sq_plane.at[q], sq_plane.at[q], plane_ss.at[SQ, d], plane_rs.at[SQ, d], plane[d])
        for d in range(Q - 1)
    ]
    for u in gram:
        finish(u, gram_gather[u])
    for copy in sq_copies:
        copy.wait_recv()
    sq_z[z] = jnp.sum(sq_plane[...], axis=0)
    sq_copies = [
        remote(sq_z.at[z], sq_z.at[z], za_ss.at[SQ, d], za_rs.at[SQ, d], line[d])
        for d in range(Z - 1)
    ]
    for u, copies in zip(proj, proj_spread):
        for copy in copies:
            copy.wait_recv()
        total = jnp.sum(spread[u - PARTS].astype(F32), axis=0)
        sums_out[1, :, columns(u)] = total / rows_total
    for copy in sq_copies:
        copy.wait_recv()
    squares = jnp.sum(jnp.sum(sq_z[...], axis=0), axis=0, keepdims=True)
    res_out[...] = jnp.sqrt(squares / rows_total)
    for copy in sends:
        copy.wait_send()


def fused_body(basis, blocks, neighbours, counts, rotation, ritz_values):
    R, Z = lax.axis_size("rows"), lax.axis_size("cols")
    nb, nnb, bs, _ = blocks.shape
    rows, k = basis.shape
    m = rotation.shape[1]
    Q, chunk, piece, wide = R // 2, k // R, k // R // Z, k // PARTS
    vmem = pltpu.VMEM
    dma = pltpu.SemaphoreType.DMA
    hbm_spec = pl.BlockSpec(memory_space=pltpu.HBM)
    vmem_spec = pl.BlockSpec(memory_space=pltpu.VMEM)
    ritz, rimg, sums, res = pl.pallas_call(
        functools.partial(kernel, (nb, nnb, bs, k, m, R, Z)),
        out_shape=(
            jax.ShapeDtypeStruct((rows, m), BF16),
            jax.ShapeDtypeStruct((rows, m), BF16),
            jax.ShapeDtypeStruct((2, chunk, k), F32),
            jax.ShapeDtypeStruct((1, m), F32),
        ),
        in_specs=[hbm_spec] * 6,
        out_specs=(vmem_spec,) * 4,
        scratch_shapes=[
            pltpu.SMEM((nb, nnb), jnp.int32),
            pltpu.SMEM((1, nb), jnp.int32),
            vmem((k, m), BF16),
            vmem((1, m), F32),
            vmem((rows, k), BF16),
            vmem((nb, nnb, bs, bs), BF16),
            vmem((rows, nb * bs), BF16),
            vmem((rows, 2 * bs), BF16),
            vmem((2 * bs, k), BF16),
            vmem((rows, k), F32),
            vmem((rows, k), BF16),
            vmem((2, k // 2, rows), BF16),
            vmem((rows, m), F32),
            vmem((2, k // 2, 2 * bs), BF16),
            vmem((PARTS, k // 2, wide), F32),
            vmem((SQ, k // 2, wide), F32),
            vmem((SQ, k // 2, wide), BF16),
            vmem((SQ, k // 2, wide), BF16),
            vmem((PARTS, chunk, wide), F32),
            vmem((SQ, Q, chunk, wide), BF16),
            vmem((SQ, Q - 1, chunk, wide), BF16),
            vmem((PARTS, Z, piece, wide), BF16),
            vmem((PARTS, Z - 1, piece, wide), BF16),
            vmem((PARTS, Z, piece, wide), BF16),
            vmem((PARTS, Z, chunk, wide), BF16),
            vmem((8, m), F32),
            vmem((8, m), F32),
            vmem((Q, 8, m), F32),
            vmem((Z, 8, m), F32),
            dma((6,)),
            dma((2,)),
            dma((2,)),
            dma((SQ + 1,)),
            dma((SQ + 1,)),
            dma((SQ + 1, Q - 1)),
            dma((SQ + 1, Q - 1)),
            dma((SQ, Z - 1)),
            dma((SQ, Z - 1)),
            dma((SQ + 1, Z - 1)),
            dma((SQ + 1, Z - 1)),
        ],
        compiler_params=pltpu.CompilerParams(
            collective_id=0, has_side_effects=True, vmem_limit_bytes=36 * 1024 * 1024
        ),
        name="davidson_step",
    )(*[
        pltpu.with_memory_space_constraint(x, pltpu.HBM)
        for x in (neighbours, counts.reshape(1, nb), basis, blocks, rotation,
                  ritz_values.reshape(1, m))
    ])
    return ritz, rimg, sums[0], sums[1], res.reshape(m)


def body(basis, blocks, neighbours, counts, rotation, ritz_values):
    R, Z = lax.axis_size("rows"), lax.axis_size("cols")
    k = basis.shape[1]
    even = R % 4 == 0 and Z > 1 and k % (16 * R * Z) == 0 and (2 * k // R) % 128 == 0
    chosen = fused_body if even else general_body
    return chosen(basis, blocks, neighbours, counts, rotation, ritz_values)


def solution(mesh):
    return jax.shard_map(
        body,
        mesh=mesh,
        in_specs=(
            P(("rows", "cols"), None),
            P(("rows", "cols"), None, None, None),
            P(("rows", "cols"), None),
            P(("rows", "cols")),
            P(),
            P(),
        ),
        out_specs=(
            P(("rows", "cols"), None),
            P(("rows", "cols"), None),
            P("rows", None),
            P("rows", None),
            P(),
        ),
        check_vma=False,
    )
```

```python
import functools

import jax
import jax.numpy as jnp
from jax import lax
from jax.experimental import pallas as pl
from jax.experimental.pallas import tpu as pltpu
from jax.sharding import PartitionSpec as P


def extended(block, sides, width):
    for axis, dim in sides:
        count = lax.axis_size(axis)
        forward = [(i, i + 1) for i in range(count - 1)]
        backward = [(target, source) for source, target in forward]
        low = lax.ppermute(
            lax.slice_in_dim(block, block.shape[dim] - width, None, axis=dim), axis, forward
        )
        high = lax.ppermute(lax.slice_in_dim(block, 0, width, axis=dim), axis, backward)
        block = jnp.concatenate([low, block, high], axis=dim)
    return block


def general_body(basis, blocks, neighbours, counts, rotation, ritz_values):
    count_blocks = blocks.shape[0]
    slots = blocks.shape[1]
    size_block = blocks.shape[2]
    width = basis.shape[1]
    devices = lax.axis_size("rows") * lax.axis_size("cols")
    rows_total = basis.shape[0] * devices
    first = lax.axis_index(("rows", "cols")) * count_blocks - 1
    local_index = neighbours - first
    live = jnp.arange(slots, dtype=jnp.int32)[None, :] < counts[:, None]
    masked = jnp.where(live[:, :, None, None], blocks, jnp.zeros_like(blocks))
    total = jnp.zeros((count_blocks, size_block, width), jnp.float32)
    own = basis.reshape(count_blocks, size_block, width)
    inside = (local_index >= 1) & (local_index <= count_blocks)
    for slot in range(slots):
        picked = own[jnp.clip(local_index[:, slot] - 1, 0, count_blocks - 1)]
        held = jnp.where(
            inside[:, slot][:, None, None], masked[:, slot], jnp.zeros_like(masked[:, slot])
        )
        total = total + jnp.einsum("brs,bsk->brk", held, picked, preferred_element_type=jnp.float32)
    padded = extended(basis, ((("rows", "cols"), 0),), size_block)
    lower_rows = padded[:size_block]
    upper_rows = padded[-size_block:]
    zero_block = jnp.zeros_like(masked)
    below = jnp.sum(jnp.where((local_index == 0)[:, :, None, None], masked, zero_block), axis=1)
    above = jnp.sum(
        jnp.where((local_index == count_blocks + 1)[:, :, None, None], masked, zero_block), axis=1
    )
    total = total + jnp.einsum("brs,sk->brk", below, lower_rows, preferred_element_type=jnp.float32)
    total = total + jnp.einsum("brs,sk->brk", above, upper_rows, preferred_element_type=jnp.float32)
    image = total.reshape(basis.shape[0], width).astype(jnp.bfloat16)
    joined = jnp.concatenate([basis, image], axis=1)
    partial_rows = lax.psum_scatter(
        jnp.dot(basis.T, joined, preferred_element_type=jnp.float32) / rows_total,
        "rows",
        scatter_dimension=0,
        tiled=True,
    )
    both = lax.psum(partial_rows.astype(jnp.bfloat16), "cols").astype(jnp.float32)
    gram = both[:, :width]
    projected = both[:, width:]
    ritz_full = jnp.dot(basis, rotation, preferred_element_type=jnp.float32)
    image_full = jnp.dot(image, rotation, preferred_element_type=jnp.float32)
    resid = image_full - ritz_values[None, :] * ritz_full
    squares = lax.psum(jnp.sum(resid * resid, axis=0), ("rows", "cols"))
    res_norm = jnp.sqrt(squares / rows_total)
    return (
        ritz_full.astype(jnp.bfloat16),
        image_full.astype(jnp.bfloat16),
        gram,
        projected,
        res_norm,
    )


BF16, F32 = jnp.bfloat16, jnp.float32
PARTS = 2
SQ = 2 * PARTS


def dot(a, b):
    return jnp.dot(a, b, preferred_element_type=F32)


def fold(x):
    return jnp.sum(x.reshape(x.shape[0] // 8, 8, x.shape[1]), axis=0)


def kernel(
    sizes, nbr_hbm, cnt_hbm, basis_hbm, blocks_hbm, rot_hbm, vals_hbm,
    ritz_v, rimg_v, sums_out, res_out,
    nbr, cnt, rot, vals,
    own, blk, mat_in, mat_halo, halo, acc, image, bt, rfull,
    reach, ready, half, core_send, core_recv, part, plane_send, plane_recv,
    z_send, z_recv, gat, sq_own, sq_core, sq_plane, sq_z,
    local_sem, halo_ss, halo_rs, core_ss, core_rs, plane_ss, plane_rs,
    zs_ss, zs_rs, za_ss, za_rs,
):
    nb, nnb, bs, k, m, R, Z = sizes
    Q = R // 2
    rows = nb * bs
    chunk = k // R
    piece = chunk // Z
    rows_total = rows * R * Z
    r = lax.axis_index("rows")
    z = lax.axis_index("cols")
    c = lax.rem(r, 2)
    q = r // 2
    me = r * Z + z
    first = me * nb - 1

    def at(index):
        return (index // Z, lax.rem(index, Z))

    ahead = at(lax.rem(me + 1, R * Z))
    behind = at(lax.rem(me + R * Z - 1, R * Z))
    mate = (q * 2 + 1 - c, z)
    plane_q = [lax.rem(q + d, Q) for d in range(1, Q)]
    plane = [(p * 2 + c, z) for p in plane_q]
    line_z = [lax.rem(z + d, Z) for d in range(1, Z)]
    line = [(r, p) for p in line_z]

    get_basis = pltpu.make_async_copy(basis_hbm, own, local_sem.at[0])
    get_basis.start()
    get_blocks = pltpu.make_async_copy(blocks_hbm, blk, local_sem.at[1])
    get_blocks.start()
    get_nbr = pltpu.make_async_copy(nbr_hbm, nbr, local_sem.at[2])
    get_nbr.start()
    get_cnt = pltpu.make_async_copy(cnt_hbm, cnt, local_sem.at[3])
    get_cnt.start()
    get_rot = pltpu.make_async_copy(rot_hbm, rot, local_sem.at[4])
    get_rot.start()
    get_vals = pltpu.make_async_copy(vals_hbm, vals, local_sem.at[5])
    get_vals.start()

    barrier = pltpu.get_barrier_semaphore()
    peers = [ahead, behind, mate] + plane + line
    for peer in peers:
        pl.semaphore_signal(barrier, inc=1, device_id=peer, device_id_type=pl.DeviceIdType.MESH)
    pl.semaphore_wait(barrier, len(peers))

    sends = []

    def remote(src, dst, ss, rs, to):
        copy = pltpu.make_async_remote_copy(
            src_ref=src, dst_ref=dst, send_sem=ss, recv_sem=rs,
            device_id=to, device_id_type=pl.DeviceIdType.MESH,
        )
        copy.start()
        sends.append(copy)
        return copy

    halo_copies = [
        remote(basis_hbm.at[pl.ds(rows - bs, bs)], halo.at[pl.ds(0, bs)],
               halo_ss.at[0], halo_rs.at[0], ahead),
        remote(basis_hbm.at[pl.ds(0, bs)], halo.at[pl.ds(bs, bs)],
               halo_ss.at[1], halo_rs.at[1], behind),
    ]

    get_basis.wait()
    for i in range(Q):
        turned = own[:, i * 2 * chunk:(i + 1) * 2 * chunk].T
        for side in range(2):
            bt[side, pl.ds(i * chunk, chunk), :] = turned[side * chunk:(side + 1) * chunk]

    wide = k // PARTS

    def columns(which):
        return pl.ds((which % PARTS) * wide, wide)

    def core_phase(which, values):
        core_send[which] = values.astype(BF16)
        return remote(core_send.at[which], core_recv.at[which], core_ss.at[which],
                      core_rs.at[which], mate)

    def plane_phase(which, core_copy):
        core_copy.wait_recv()
        total = half[which] + core_recv[which].astype(F32)
        half[which] = total
        plane_send[which] = total.astype(BF16).reshape(Q, chunk, wide)
        return [
            remote(plane_send.at[which, plane_q[d]], plane_recv.at[which, d],
                   plane_ss.at[which, d], plane_rs.at[which, d], plane[d])
            for d in range(Q - 1)
        ]

    def line_phase(which, copies):
        total = half[which, pl.ds(pl.multiple_of(q * chunk, chunk), chunk), :]
        for d, copy in enumerate(copies):
            copy.wait_recv()
            total = total + plane_recv[which, d].astype(F32)
        part[which] = total
        z_send[which] = total.astype(BF16).reshape(Z, piece, wide)
        return [
            remote(z_send.at[which, line_z[d]], z_recv.at[which, d],
                   zs_ss.at[which, d], zs_rs.at[which, d], line[d])
            for d in range(Z - 1)
        ]

    def gather_phase(which, copies):
        total = part[which, pl.ds(pl.multiple_of(z * piece, piece), piece), :]
        for d, copy in enumerate(copies):
            copy.wait_recv()
            total = total + z_recv[which, d].astype(F32)
        gat[which, z] = total.astype(BF16)
        return [
            remote(gat.at[which, z], gat.at[which, z],
                   za_ss.at[which, d], za_rs.at[which, d], line[d])
            for d in range(Z - 1)
        ]

    def finish(which, copies):
        for copy in copies:
            copy.wait_recv()
        sums_out[which // PARTS, :, columns(which)] = (
            gat[which].astype(F32).reshape(chunk, wide) / rows_total
        )

    gram = range(PARTS)
    proj = range(PARTS, 2 * PARTS)

    def both_halves(which, right):
        left = bt[...].reshape(k, rows)
        ready[which] = dot(left, right[:, columns(which)]).reshape(2, k // 2, wide)

    gram_core = []
    for u in gram:
        both_halves(u, own)
        gram_core.append(core_phase(u, ready[u, 1 - c]))
        half[u] = ready[u, c]

    get_rot.wait()
    rfull[...] = dot(own[...], rot[...])
    ritz_v[...] = rfull[...].astype(BF16)

    gram_plane = [plane_phase(u, gram_core[u]) for u in gram]

    get_blocks.wait()
    get_nbr.wait()
    get_cnt.wait()

    @pl.loop(0, nb)
    def _(b):
        n = cnt[0, b]
        spot = [jnp.where(j < n, nbr[b, j] - first, -1) for j in range(nnb)]
        tiles = [blk[b, j] for j in range(nnb)]
        there = pl.ds(pl.multiple_of(b * bs, bs), bs)
        for s in range(nb + 2):
            total = jnp.zeros((bs, bs), BF16)
            for j in range(nnb):
                weight = jnp.where(spot[j] == s, 1.0, 0.0).astype(F32)
                total = total + tiles[j] * jnp.full((bs, bs), weight, F32).astype(BF16)
            if s == 0:
                mat_halo[there, 0:bs] = total
            elif s == nb + 1:
                mat_halo[there, bs:2 * bs] = total
            else:
                mat_in[there, (s - 1) * bs:s * bs] = total


    step = min(rows, 4 * bs)

    @pl.loop(0, rows // step)
    def _(i):
        there = pl.ds(pl.multiple_of(i * step, step), step)
        inside = dot(mat_in[there, :], own[...])
        acc[there, :] = inside
        image[there, :] = inside.astype(BF16)

    reach[...] = dot(bt[...].reshape(k, rows), mat_halo[...]).astype(BF16).reshape(reach.shape)
    for u in proj:
        both_halves(u, image)

    for copy in halo_copies:
        copy.wait_recv()

    proj_core = [
        core_phase(u, ready[u, 1 - c] + dot(reach[1 - c], halo[:, columns(u)])) for u in proj
    ]
    for u in proj:
        half[u] = ready[u, c] + dot(reach[c], halo[:, columns(u)])
    gram_line = [line_phase(u, gram_plane[u]) for u in gram]
    proj_plane = [plane_phase(u, copy) for u, copy in zip(proj, proj_core)]
    get_vals.wait()

    sq_own[...] = jnp.zeros_like(sq_own)

    @pl.loop(0, rows // step)
    def _(i):
        there = pl.ds(pl.multiple_of(i * step, step), step)
        outside = dot(mat_halo[there, :], halo[...])
        full = dot((acc[there, :] + outside).astype(BF16), rot[...])
        rimg_v[there, :] = full.astype(BF16)
        resid = full - vals[...] * rfull[there, :]
        sq_own[...] += fold(resid * resid)

    sq_copy = remote(sq_own, sq_core, core_ss.at[SQ], core_rs.at[SQ], mate)

    gram_gather = [gather_phase(u, gram_line[u]) for u in gram]
    proj_line = [line_phase(u, copies) for u, copies in zip(proj, proj_plane)]
    sq_copy.wait_recv()
    sq_plane[q] = sq_own[...] + sq_core[...]
    sq_copies = [
        remote(sq_plane.at[q], sq_plane.at[q], plane_ss.at[SQ, d], plane_rs.at[SQ, d], plane[d])
        for d in range(Q - 1)
    ]
    for u in gram:
        finish(u, gram_gather[u])
    proj_gather = [gather_phase(u, copies) for u, copies in zip(proj, proj_line)]
    for copy in sq_copies:
        copy.wait_recv()
    sq_z[z] = jnp.sum(sq_plane[...], axis=0)
    sq_copies = [
        remote(sq_z.at[z], sq_z.at[z], za_ss.at[SQ, d], za_rs.at[SQ, d], line[d])
        for d in range(Z - 1)
    ]
    for u, copies in zip(proj, proj_gather):
        finish(u, copies)
    for copy in sq_copies:
        copy.wait_recv()
    squares = jnp.sum(jnp.sum(sq_z[...], axis=0), axis=0, keepdims=True)
    res_out[...] = jnp.sqrt(squares / rows_total)
    for copy in sends:
        copy.wait_send()


def fused_body(basis, blocks, neighbours, counts, rotation, ritz_values):
    R, Z = lax.axis_size("rows"), lax.axis_size("cols")
    nb, nnb, bs, _ = blocks.shape
    rows, k = basis.shape
    m = rotation.shape[1]
    Q, chunk, piece, wide = R // 2, k // R, k // R // Z, k // PARTS
    vmem = pltpu.VMEM
    dma = pltpu.SemaphoreType.DMA
    hbm_spec = pl.BlockSpec(memory_space=pltpu.HBM)
    vmem_spec = pl.BlockSpec(memory_space=pltpu.VMEM)
    ritz, rimg, sums, res = pl.pallas_call(
        functools.partial(kernel, (nb, nnb, bs, k, m, R, Z)),
        out_shape=(
            jax.ShapeDtypeStruct((rows, m), BF16),
            jax.ShapeDtypeStruct((rows, m), BF16),
            jax.ShapeDtypeStruct((2, chunk, k), F32),
            jax.ShapeDtypeStruct((1, m), F32),
        ),
        in_specs=[hbm_spec] * 6,
        out_specs=(vmem_spec,) * 4,
        scratch_shapes=[
            pltpu.SMEM((nb, nnb), jnp.int32),
            pltpu.SMEM((1, nb), jnp.int32),
            vmem((k, m), BF16),
            vmem((1, m), F32),
            vmem((rows, k), BF16),
            vmem((nb, nnb, bs, bs), BF16),
            vmem((rows, nb * bs), BF16),
            vmem((rows, 2 * bs), BF16),
            vmem((2 * bs, k), BF16),
            vmem((rows, k), F32),
            vmem((rows, k), BF16),
            vmem((2, k // 2, rows), BF16),
            vmem((rows, m), F32),
            vmem((2, k // 2, 2 * bs), BF16),
            vmem((SQ, 2, k // 2, wide), F32),
            vmem((SQ, k // 2, wide), F32),
            vmem((SQ, k // 2, wide), BF16),
            vmem((SQ, k // 2, wide), BF16),
            vmem((SQ, chunk, wide), F32),
            vmem((SQ, Q, chunk, wide), BF16),
            vmem((SQ, Q - 1, chunk, wide), BF16),
            vmem((SQ, Z, piece, wide), BF16),
            vmem((SQ, Z - 1, piece, wide), BF16),
            vmem((SQ, Z, piece, wide), BF16),
            vmem((8, m), F32),
            vmem((8, m), F32),
            vmem((Q, 8, m), F32),
            vmem((Z, 8, m), F32),
            dma((6,)),
            dma((2,)),
            dma((2,)),
            dma((SQ + 1,)),
            dma((SQ + 1,)),
            dma((SQ + 1, Q - 1)),
            dma((SQ + 1, Q - 1)),
            dma((SQ, Z - 1)),
            dma((SQ, Z - 1)),
            dma((SQ + 1, Z - 1)),
            dma((SQ + 1, Z - 1)),
        ],
        compiler_params=pltpu.CompilerParams(
            collective_id=0, has_side_effects=True, vmem_limit_bytes=36 * 1024 * 1024
        ),
        name="davidson_step",
    )(*[
        pltpu.with_memory_space_constraint(x, pltpu.HBM)
        for x in (neighbours, counts.reshape(1, nb), basis, blocks, rotation,
                  ritz_values.reshape(1, m))
    ])
    return ritz, rimg, sums[0], sums[1], res.reshape(m)


def body(basis, blocks, neighbours, counts, rotation, ritz_values):
    R, Z = lax.axis_size("rows"), lax.axis_size("cols")
    k = basis.shape[1]
    even = R % 4 == 0 and Z > 1 and k % (16 * R * Z) == 0 and (2 * k // R) % 128 == 0
    even = even and blocks.shape[0] % 4 == 0 and k % (256 * PARTS) == 0
    chosen = fused_body if even else general_body
    return chosen(basis, blocks, neighbours, counts, rotation, ritz_values)


def solution(mesh):
    return jax.shard_map(
        body,
        mesh=mesh,
        in_specs=(
            P(("rows", "cols"), None),
            P(("rows", "cols"), None, None, None),
            P(("rows", "cols"), None),
            P(("rows", "cols")),
            P(),
            P(),
        ),
        out_specs=(
            P(("rows", "cols"), None),
            P(("rows", "cols"), None),
            P("rows", None),
            P("rows", None),
            P(),
        ),
        check_vma=False,
    )
```

```python
import functools

import jax
import jax.numpy as jnp
from jax import lax
from jax.experimental import pallas as pl
from jax.experimental.pallas import tpu as pltpu
from jax.sharding import PartitionSpec as P


def extended(block, sides, width):
    for axis, dim in sides:
        count = lax.axis_size(axis)
        forward = [(i, i + 1) for i in range(count - 1)]
        backward = [(target, source) for source, target in forward]
        low = lax.ppermute(
            lax.slice_in_dim(block, block.shape[dim] - width, None, axis=dim), axis, forward
        )
        high = lax.ppermute(lax.slice_in_dim(block, 0, width, axis=dim), axis, backward)
        block = jnp.concatenate([low, block, high], axis=dim)
    return block


def general_body(basis, blocks, neighbours, counts, rotation, ritz_values):
    count_blocks = blocks.shape[0]
    slots = blocks.shape[1]
    size_block = blocks.shape[2]
    width = basis.shape[1]
    devices = lax.axis_size("rows") * lax.axis_size("cols")
    rows_total = basis.shape[0] * devices
    first = lax.axis_index(("rows", "cols")) * count_blocks - 1
    local_index = neighbours - first
    live = jnp.arange(slots, dtype=jnp.int32)[None, :] < counts[:, None]
    masked = jnp.where(live[:, :, None, None], blocks, jnp.zeros_like(blocks))
    total = jnp.zeros((count_blocks, size_block, width), jnp.float32)
    own = basis.reshape(count_blocks, size_block, width)
    inside = (local_index >= 1) & (local_index <= count_blocks)
    for slot in range(slots):
        picked = own[jnp.clip(local_index[:, slot] - 1, 0, count_blocks - 1)]
        held = jnp.where(
            inside[:, slot][:, None, None], masked[:, slot], jnp.zeros_like(masked[:, slot])
        )
        total = total + jnp.einsum("brs,bsk->brk", held, picked, preferred_element_type=jnp.float32)
    padded = extended(basis, ((("rows", "cols"), 0),), size_block)
    lower_rows = padded[:size_block]
    upper_rows = padded[-size_block:]
    zero_block = jnp.zeros_like(masked)
    below = jnp.sum(jnp.where((local_index == 0)[:, :, None, None], masked, zero_block), axis=1)
    above = jnp.sum(
        jnp.where((local_index == count_blocks + 1)[:, :, None, None], masked, zero_block), axis=1
    )
    total = total + jnp.einsum("brs,sk->brk", below, lower_rows, preferred_element_type=jnp.float32)
    total = total + jnp.einsum("brs,sk->brk", above, upper_rows, preferred_element_type=jnp.float32)
    image = total.reshape(basis.shape[0], width).astype(jnp.bfloat16)
    joined = jnp.concatenate([basis, image], axis=1)
    partial_rows = lax.psum_scatter(
        jnp.dot(basis.T, joined, preferred_element_type=jnp.float32) / rows_total,
        "rows",
        scatter_dimension=0,
        tiled=True,
    )
    both = lax.psum(partial_rows.astype(jnp.bfloat16), "cols").astype(jnp.float32)
    gram = both[:, :width]
    projected = both[:, width:]
    ritz_full = jnp.dot(basis, rotation, preferred_element_type=jnp.float32)
    image_full = jnp.dot(image, rotation, preferred_element_type=jnp.float32)
    resid = image_full - ritz_values[None, :] * ritz_full
    squares = lax.psum(jnp.sum(resid * resid, axis=0), ("rows", "cols"))
    res_norm = jnp.sqrt(squares / rows_total)
    return (
        ritz_full.astype(jnp.bfloat16),
        image_full.astype(jnp.bfloat16),
        gram,
        projected,
        res_norm,
    )


BF16, F32 = jnp.bfloat16, jnp.float32
PARTS = 2
SQ = 2 * PARTS


def dot(a, b):
    return jnp.dot(a, b, preferred_element_type=F32)


def fold(x):
    return jnp.sum(x.reshape(x.shape[0] // 8, 8, x.shape[1]), axis=0)


def kernel(
    sizes, nbr_hbm, cnt_hbm, basis_hbm, blocks_hbm, rot_hbm, vals_hbm,
    ritz_v, rimg_v, sums_out, res_out,
    nbr, cnt, rot, vals,
    own, blk, mat_in, mat_halo, halo, acc, image, bt, rfull,
    reach, ready, half, core_send, core_recv, part, plane_send, plane_recv,
    z_send, z_recv, gat, sq_own, sq_core, sq_plane, sq_z,
    local_sem, halo_ss, halo_rs, core_ss, core_rs, plane_ss, plane_rs,
    zs_ss, zs_rs, za_ss, za_rs,
):
    nb, nnb, bs, k, m, R, Z = sizes
    Q = R // 2
    rows = nb * bs
    chunk = k // R
    piece = chunk // Z
    rows_total = rows * R * Z
    r = lax.axis_index("rows")
    z = lax.axis_index("cols")
    c = lax.rem(r, 2)
    q = r // 2
    me = r * Z + z
    first = me * nb - 1

    def at(index):
        return (index // Z, lax.rem(index, Z))

    ahead = at(lax.rem(me + 1, R * Z))
    behind = at(lax.rem(me + R * Z - 1, R * Z))
    mate = (q * 2 + 1 - c, z)
    plane_q = [lax.rem(q + d, Q) for d in range(1, Q)]
    plane = [(p * 2 + c, z) for p in plane_q]
    line_z = [lax.rem(z + d, Z) for d in range(1, Z)]
    line = [(r, p) for p in line_z]

    get_basis = pltpu.make_async_copy(basis_hbm, own, local_sem.at[0])
    get_basis.start()
    get_blocks = pltpu.make_async_copy(blocks_hbm, blk, local_sem.at[1])
    get_blocks.start()
    get_nbr = pltpu.make_async_copy(nbr_hbm, nbr, local_sem.at[2])
    get_nbr.start()
    get_cnt = pltpu.make_async_copy(cnt_hbm, cnt, local_sem.at[3])
    get_cnt.start()
    get_rot = pltpu.make_async_copy(rot_hbm, rot, local_sem.at[4])
    get_rot.start()
    get_vals = pltpu.make_async_copy(vals_hbm, vals, local_sem.at[5])
    get_vals.start()

    barrier = pltpu.get_barrier_semaphore()
    peers = [ahead, behind, mate] + plane + line
    for peer in peers:
        pl.semaphore_signal(barrier, inc=1, device_id=peer, device_id_type=pl.DeviceIdType.MESH)
    pl.semaphore_wait(barrier, len(peers))

    sends = []

    def remote(src, dst, ss, rs, to):
        copy = pltpu.make_async_remote_copy(
            src_ref=src, dst_ref=dst, send_sem=ss, recv_sem=rs,
            device_id=to, device_id_type=pl.DeviceIdType.MESH,
        )
        copy.start()
        sends.append(copy)
        return copy

    halo_copies = [
        remote(basis_hbm.at[pl.ds(rows - bs, bs)], halo.at[pl.ds(0, bs)],
               halo_ss.at[0], halo_rs.at[0], ahead),
        remote(basis_hbm.at[pl.ds(0, bs)], halo.at[pl.ds(bs, bs)],
               halo_ss.at[1], halo_rs.at[1], behind),
    ]

    get_basis.wait()
    for i in range(Q):
        turned = own[:, i * 2 * chunk:(i + 1) * 2 * chunk].T
        for side in range(2):
            bt[side, pl.ds(i * chunk, chunk), :] = turned[side * chunk:(side + 1) * chunk]

    wide = k // PARTS

    def columns(which):
        return pl.ds((which % PARTS) * wide, wide)

    def core_phase(which, values):
        core_send[which] = values.astype(BF16)
        return remote(core_send.at[which], core_recv.at[which], core_ss.at[which],
                      core_rs.at[which], mate)

    def plane_phase(which, core_copy):
        core_copy.wait_recv()
        total = half[which] + core_recv[which].astype(F32)
        half[which] = total
        plane_send[which] = total.astype(BF16).reshape(Q, chunk, wide)
        return [
            remote(plane_send.at[which, plane_q[d]], plane_recv.at[which, d],
                   plane_ss.at[which, d], plane_rs.at[which, d], plane[d])
            for d in range(Q - 1)
        ]

    def line_phase(which, copies):
        total = half[which, pl.ds(pl.multiple_of(q * chunk, chunk), chunk), :]
        for d, copy in enumerate(copies):
            copy.wait_recv()
            total = total + plane_recv[which, d].astype(F32)
        part[which] = total
        z_send[which] = total.astype(BF16).reshape(Z, piece, wide)
        return [
            remote(z_send.at[which, line_z[d]], z_recv.at[which, d],
                   zs_ss.at[which, d], zs_rs.at[which, d], line[d])
            for d in range(Z - 1)
        ]

    def gather_phase(which, copies):
        total = part[which, pl.ds(pl.multiple_of(z * piece, piece), piece), :]
        for d, copy in enumerate(copies):
            copy.wait_recv()
            total = total + z_recv[which, d].astype(F32)
        gat[which, z] = total.astype(BF16)
        return [
            remote(gat.at[which, z], gat.at[which, z],
                   za_ss.at[which, d], za_rs.at[which, d], line[d])
            for d in range(Z - 1)
        ]

    def finish(which, copies):
        for copy in copies:
            copy.wait_recv()
        sums_out[which // PARTS, :, columns(which)] = (
            gat[which].astype(F32).reshape(chunk, wide) / rows_total
        )

    gram = range(PARTS)
    proj = range(PARTS, 2 * PARTS)

    gram_core = [core_phase(u, dot(bt[1 - c], own[:, columns(u)])) for u in gram]
    for u in gram:
        half[u] = dot(bt[c], own[:, columns(u)])

    get_rot.wait()
    rfull[...] = dot(own[...], rot[...])
    ritz_v[...] = rfull[...].astype(BF16)

    gram_plane = [plane_phase(u, gram_core[u]) for u in gram]

    get_blocks.wait()
    get_nbr.wait()
    get_cnt.wait()

    @pl.loop(0, nb)
    def _(b):
        n = cnt[0, b]
        spot = [jnp.where(j < n, nbr[b, j] - first, -1) for j in range(nnb)]
        tiles = [blk[b, j] for j in range(nnb)]
        there = pl.ds(pl.multiple_of(b * bs, bs), bs)
        for s in range(nb + 2):
            total = jnp.zeros((bs, bs), BF16)
            for j in range(nnb):
                weight = jnp.where(spot[j] == s, 1.0, 0.0).astype(F32)
                total = total + tiles[j] * jnp.full((bs, bs), weight, F32).astype(BF16)
            if s == 0:
                mat_halo[there, 0:bs] = total
            elif s == nb + 1:
                mat_halo[there, bs:2 * bs] = total
            else:
                mat_in[there, (s - 1) * bs:s * bs] = total


    step = min(rows, 2 * bs)

    @pl.loop(0, rows // step)
    def _(i):
        there = pl.ds(pl.multiple_of(i * step, step), step)
        inside = dot(mat_in[there, :], own[...])
        acc[there, :] = inside
        image[there, :] = inside.astype(BF16)

    for side in range(2):
        reach[side] = dot(bt[side], mat_halo[...]).astype(BF16)
    for u in proj:
        ready[u - PARTS] = dot(bt[1 - c], image[:, columns(u)])
    for u in proj:
        half[u] = dot(bt[c], image[:, columns(u)])

    for copy in halo_copies:
        copy.wait_recv()

    proj_core = [
        core_phase(u, ready[u - PARTS] + dot(reach[1 - c], halo[:, columns(u)])) for u in proj
    ]
    gram_line = [line_phase(u, gram_plane[u]) for u in gram]
    for u in proj:
        half[u] += dot(reach[c], halo[:, columns(u)])
    proj_plane = [plane_phase(u, copy) for u, copy in zip(proj, proj_core)]
    get_vals.wait()

    sq_own[...] = jnp.zeros_like(sq_own)

    def rotate(i):
        there = pl.ds(pl.multiple_of(i * step, step), step)
        outside = dot(mat_halo[there, :], halo[...])
        full = dot((acc[there, :] + outside).astype(BF16), rot[...])
        rimg_v[there, :] = full.astype(BF16)
        resid = full - vals[...] * rfull[there, :]
        sq_own[...] += fold(resid * resid)

    middle = rows // step // 2
    pl.loop(0, middle)(rotate)
    gram_gather = [gather_phase(u, gram_line[u]) for u in gram]
    pl.loop(middle, rows // step)(rotate)

    sq_copy = remote(sq_own, sq_core, core_ss.at[SQ], core_rs.at[SQ], mate)

    proj_line = [line_phase(u, copies) for u, copies in zip(proj, proj_plane)]
    sq_copy.wait_recv()
    sq_plane[q] = sq_own[...] + sq_core[...]
    sq_copies = [
        remote(sq_plane.at[q], sq_plane.at[q], plane_ss.at[SQ, d], plane_rs.at[SQ, d], plane[d])
        for d in range(Q - 1)
    ]
    for u in gram:
        finish(u, gram_gather[u])
    proj_gather = [gather_phase(u, copies) for u, copies in zip(proj, proj_line)]
    for copy in sq_copies:
        copy.wait_recv()
    sq_z[z] = jnp.sum(sq_plane[...], axis=0)
    sq_copies = [
        remote(sq_z.at[z], sq_z.at[z], za_ss.at[SQ, d], za_rs.at[SQ, d], line[d])
        for d in range(Z - 1)
    ]
    for u, copies in zip(proj, proj_gather):
        finish(u, copies)
    for copy in sq_copies:
        copy.wait_recv()
    squares = jnp.sum(jnp.sum(sq_z[...], axis=0), axis=0, keepdims=True)
    res_out[...] = jnp.sqrt(squares / rows_total)
    for copy in sends:
        copy.wait_send()


def fused_body(basis, blocks, neighbours, counts, rotation, ritz_values):
    R, Z = lax.axis_size("rows"), lax.axis_size("cols")
    nb, nnb, bs, _ = blocks.shape
    rows, k = basis.shape
    m = rotation.shape[1]
    Q, chunk, piece, wide = R // 2, k // R, k // R // Z, k // PARTS
    vmem = pltpu.VMEM
    dma = pltpu.SemaphoreType.DMA
    hbm_spec = pl.BlockSpec(memory_space=pltpu.HBM)
    vmem_spec = pl.BlockSpec(memory_space=pltpu.VMEM)
    ritz, rimg, sums, res = pl.pallas_call(
        functools.partial(kernel, (nb, nnb, bs, k, m, R, Z)),
        out_shape=(
            jax.ShapeDtypeStruct((rows, m), BF16),
            jax.ShapeDtypeStruct((rows, m), BF16),
            jax.ShapeDtypeStruct((2, chunk, k), F32),
            jax.ShapeDtypeStruct((1, m), F32),
        ),
        in_specs=[hbm_spec] * 6,
        out_specs=(vmem_spec,) * 4,
        scratch_shapes=[
            pltpu.SMEM((nb, nnb), jnp.int32),
            pltpu.SMEM((1, nb), jnp.int32),
            vmem((k, m), BF16),
            vmem((1, m), F32),
            vmem((rows, k), BF16),
            vmem((nb, nnb, bs, bs), BF16),
            vmem((rows, nb * bs), BF16),
            vmem((rows, 2 * bs), BF16),
            vmem((2 * bs, k), BF16),
            vmem((rows, k), F32),
            vmem((rows, k), BF16),
            vmem((2, k // 2, rows), BF16),
            vmem((rows, m), F32),
            vmem((2, k // 2, 2 * bs), BF16),
            vmem((PARTS, k // 2, wide), F32),
            vmem((SQ, k // 2, wide), F32),
            vmem((SQ, k // 2, wide), BF16),
            vmem((SQ, k // 2, wide), BF16),
            vmem((SQ, chunk, wide), F32),
            vmem((SQ, Q, chunk, wide), BF16),
            vmem((SQ, Q - 1, chunk, wide), BF16),
            vmem((SQ, Z, piece, wide), BF16),
            vmem((SQ, Z - 1, piece, wide), BF16),
            vmem((SQ, Z, piece, wide), BF16),
            vmem((8, m), F32),
            vmem((8, m), F32),
            vmem((Q, 8, m), F32),
            vmem((Z, 8, m), F32),
            dma((6,)),
            dma((2,)),
            dma((2,)),
            dma((SQ + 1,)),
            dma((SQ + 1,)),
            dma((SQ + 1, Q - 1)),
            dma((SQ + 1, Q - 1)),
            dma((SQ, Z - 1)),
            dma((SQ, Z - 1)),
            dma((SQ + 1, Z - 1)),
            dma((SQ + 1, Z - 1)),
        ],
        compiler_params=pltpu.CompilerParams(
            collective_id=0, has_side_effects=True, vmem_limit_bytes=36 * 1024 * 1024
        ),
        name="davidson_step",
    )(*[
        pltpu.with_memory_space_constraint(x, pltpu.HBM)
        for x in (neighbours, counts.reshape(1, nb), basis, blocks, rotation,
                  ritz_values.reshape(1, m))
    ])
    return ritz, rimg, sums[0], sums[1], res.reshape(m)


def body(basis, blocks, neighbours, counts, rotation, ritz_values):
    R, Z = lax.axis_size("rows"), lax.axis_size("cols")
    k = basis.shape[1]
    even = R % 4 == 0 and Z > 1 and k % (16 * R * Z) == 0 and (2 * k // R) % 128 == 0
    chosen = fused_body if even else general_body
    return chosen(basis, blocks, neighbours, counts, rotation, ritz_values)


def solution(mesh):
    return jax.shard_map(
        body,
        mesh=mesh,
        in_specs=(
            P(("rows", "cols"), None),
            P(("rows", "cols"), None, None, None),
            P(("rows", "cols"), None),
            P(("rows", "cols")),
            P(),
            P(),
        ),
        out_specs=(
            P(("rows", "cols"), None),
            P(("rows", "cols"), None),
            P("rows", None),
            P("rows", None),
            P(),
        ),
        check_vma=False,
    )
```

```python
import functools

import jax
import jax.numpy as jnp
from jax import lax
from jax.experimental import pallas as pl
from jax.experimental.pallas import tpu as pltpu
from jax.sharding import PartitionSpec as P


def extended(block, sides, width):
    for axis, dim in sides:
        count = lax.axis_size(axis)
        forward = [(i, i + 1) for i in range(count - 1)]
        backward = [(target, source) for source, target in forward]
        low = lax.ppermute(
            lax.slice_in_dim(block, block.shape[dim] - width, None, axis=dim), axis, forward
        )
        high = lax.ppermute(lax.slice_in_dim(block, 0, width, axis=dim), axis, backward)
        block = jnp.concatenate([low, block, high], axis=dim)
    return block


def general_body(basis, blocks, neighbours, counts, rotation, ritz_values):
    count_blocks = blocks.shape[0]
    slots = blocks.shape[1]
    size_block = blocks.shape[2]
    width = basis.shape[1]
    devices = lax.axis_size("rows") * lax.axis_size("cols")
    rows_total = basis.shape[0] * devices
    first = lax.axis_index(("rows", "cols")) * count_blocks - 1
    local_index = neighbours - first
    live = jnp.arange(slots, dtype=jnp.int32)[None, :] < counts[:, None]
    masked = jnp.where(live[:, :, None, None], blocks, jnp.zeros_like(blocks))
    total = jnp.zeros((count_blocks, size_block, width), jnp.float32)
    own = basis.reshape(count_blocks, size_block, width)
    inside = (local_index >= 1) & (local_index <= count_blocks)
    for slot in range(slots):
        picked = own[jnp.clip(local_index[:, slot] - 1, 0, count_blocks - 1)]
        held = jnp.where(
            inside[:, slot][:, None, None], masked[:, slot], jnp.zeros_like(masked[:, slot])
        )
        total = total + jnp.einsum("brs,bsk->brk", held, picked, preferred_element_type=jnp.float32)
    padded = extended(basis, ((("rows", "cols"), 0),), size_block)
    lower_rows = padded[:size_block]
    upper_rows = padded[-size_block:]
    zero_block = jnp.zeros_like(masked)
    below = jnp.sum(jnp.where((local_index == 0)[:, :, None, None], masked, zero_block), axis=1)
    above = jnp.sum(
        jnp.where((local_index == count_blocks + 1)[:, :, None, None], masked, zero_block), axis=1
    )
    total = total + jnp.einsum("brs,sk->brk", below, lower_rows, preferred_element_type=jnp.float32)
    total = total + jnp.einsum("brs,sk->brk", above, upper_rows, preferred_element_type=jnp.float32)
    image = total.reshape(basis.shape[0], width).astype(jnp.bfloat16)
    joined = jnp.concatenate([basis, image], axis=1)
    partial_rows = lax.psum_scatter(
        jnp.dot(basis.T, joined, preferred_element_type=jnp.float32) / rows_total,
        "rows",
        scatter_dimension=0,
        tiled=True,
    )
    both = lax.psum(partial_rows.astype(jnp.bfloat16), "cols").astype(jnp.float32)
    gram = both[:, :width]
    projected = both[:, width:]
    ritz_full = jnp.dot(basis, rotation, preferred_element_type=jnp.float32)
    image_full = jnp.dot(image, rotation, preferred_element_type=jnp.float32)
    resid = image_full - ritz_values[None, :] * ritz_full
    squares = lax.psum(jnp.sum(resid * resid, axis=0), ("rows", "cols"))
    res_norm = jnp.sqrt(squares / rows_total)
    return (
        ritz_full.astype(jnp.bfloat16),
        image_full.astype(jnp.bfloat16),
        gram,
        projected,
        res_norm,
    )


BF16, F32 = jnp.bfloat16, jnp.float32
PARTS = 1
SQ = 2 * PARTS


def dot(a, b):
    return jnp.dot(a, b, preferred_element_type=F32)


def fold(x):
    return jnp.sum(x.reshape(x.shape[0] // 8, 8, x.shape[1]), axis=0)


def kernel(
    sizes, nbr_hbm, cnt_hbm, basis_hbm, blocks_hbm, rot_hbm, vals_hbm,
    ritz_v, rimg_v, sums_out, res_out,
    nbr, cnt, rot, vals,
    own, blk, mat_in, mat_halo, halo, acc, image, bt, rfull,
    reach, ready, half, core_send, core_recv, part, plane_send, plane_recv,
    z_send, z_recv, gat, sq_own, sq_core, sq_plane, sq_z,
    local_sem, halo_ss, halo_rs, core_ss, core_rs, plane_ss, plane_rs,
    zs_ss, zs_rs, za_ss, za_rs,
):
    nb, nnb, bs, k, m, R, Z = sizes
    Q = R // 2
    rows = nb * bs
    chunk = k // R
    piece = chunk // Z
    rows_total = rows * R * Z
    r = lax.axis_index("rows")
    z = lax.axis_index("cols")
    c = lax.rem(r, 2)
    q = r // 2
    me = r * Z + z
    first = me * nb - 1

    def at(index):
        return (index // Z, lax.rem(index, Z))

    ahead = at(lax.rem(me + 1, R * Z))
    behind = at(lax.rem(me + R * Z - 1, R * Z))
    mate = (q * 2 + 1 - c, z)
    plane_q = [lax.rem(q + d, Q) for d in range(1, Q)]
    plane = [(p * 2 + c, z) for p in plane_q]
    line_z = [lax.rem(z + d, Z) for d in range(1, Z)]
    line = [(r, p) for p in line_z]

    get_basis = pltpu.make_async_copy(basis_hbm, own, local_sem.at[0])
    get_basis.start()
    get_blocks = pltpu.make_async_copy(blocks_hbm, blk, local_sem.at[1])
    get_blocks.start()
    get_nbr = pltpu.make_async_copy(nbr_hbm, nbr, local_sem.at[2])
    get_nbr.start()
    get_cnt = pltpu.make_async_copy(cnt_hbm, cnt, local_sem.at[3])
    get_cnt.start()
    get_rot = pltpu.make_async_copy(rot_hbm, rot, local_sem.at[4])
    get_rot.start()
    get_vals = pltpu.make_async_copy(vals_hbm, vals, local_sem.at[5])
    get_vals.start()

    barrier = pltpu.get_barrier_semaphore()
    peers = [ahead, behind, mate] + plane + line
    for peer in peers:
        pl.semaphore_signal(barrier, inc=1, device_id=peer, device_id_type=pl.DeviceIdType.MESH)
    pl.semaphore_wait(barrier, len(peers))

    sends = []

    def remote(src, dst, ss, rs, to):
        copy = pltpu.make_async_remote_copy(
            src_ref=src, dst_ref=dst, send_sem=ss, recv_sem=rs,
            device_id=to, device_id_type=pl.DeviceIdType.MESH,
        )
        copy.start()
        sends.append(copy)
        return copy

    halo_copies = [
        remote(basis_hbm.at[pl.ds(rows - bs, bs)], halo.at[pl.ds(0, bs)],
               halo_ss.at[0], halo_rs.at[0], ahead),
        remote(basis_hbm.at[pl.ds(0, bs)], halo.at[pl.ds(bs, bs)],
               halo_ss.at[1], halo_rs.at[1], behind),
    ]

    get_basis.wait()
    for i in range(Q):
        turned = own[:, i * 2 * chunk:(i + 1) * 2 * chunk].T
        for side in range(2):
            bt[side, pl.ds(i * chunk, chunk), :] = turned[side * chunk:(side + 1) * chunk]

    wide = k // PARTS

    def columns(which):
        return pl.ds((which % PARTS) * wide, wide)

    def core_phase(which, values):
        core_send[which] = values.astype(BF16)
        return remote(core_send.at[which], core_recv.at[which], core_ss.at[which],
                      core_rs.at[which], mate)

    def plane_phase(which, core_copy):
        core_copy.wait_recv()
        total = half[which] + core_recv[which].astype(F32)
        half[which] = total
        plane_send[which] = total.astype(BF16).reshape(Q, chunk, wide)
        return [
            remote(plane_send.at[which, plane_q[d]], plane_recv.at[which, d],
                   plane_ss.at[which, d], plane_rs.at[which, d], plane[d])
            for d in range(Q - 1)
        ]

    def line_phase(which, copies):
        total = half[which, pl.ds(pl.multiple_of(q * chunk, chunk), chunk), :]
        for d, copy in enumerate(copies):
            copy.wait_recv()
            total = total + plane_recv[which, d].astype(F32)
        part[which] = total
        z_send[which] = total.astype(BF16).reshape(Z, piece, wide)
        return [
            remote(z_send.at[which, line_z[d]], z_recv.at[which, d],
                   zs_ss.at[which, d], zs_rs.at[which, d], line[d])
            for d in range(Z - 1)
        ]

    def gather_phase(which, copies):
        total = part[which, pl.ds(pl.multiple_of(z * piece, piece), piece), :]
        for d, copy in enumerate(copies):
            copy.wait_recv()
            total = total + z_recv[which, d].astype(F32)
        gat[which, z] = total.astype(BF16)
        return [
            remote(gat.at[which, z], gat.at[which, z],
                   za_ss.at[which, d], za_rs.at[which, d], line[d])
            for d in range(Z - 1)
        ]

    def finish(which, copies):
        for copy in copies:
            copy.wait_recv()
        sums_out[which // PARTS, :, columns(which)] = (
            gat[which].astype(F32).reshape(chunk, wide) / rows_total
        )

    gram = range(PARTS)
    proj = range(PARTS, 2 * PARTS)

    gram_core = [core_phase(u, dot(bt[1 - c], own[:, columns(u)])) for u in gram]
    for u in gram:
        half[u] = dot(bt[c], own[:, columns(u)])

    get_rot.wait()
    rfull[...] = dot(own[...], rot[...])
    ritz_v[...] = rfull[...].astype(BF16)

    gram_plane = [plane_phase(u, gram_core[u]) for u in gram]

    get_blocks.wait()
    get_nbr.wait()
    get_cnt.wait()

    @pl.loop(0, nb)
    def _(b):
        n = cnt[0, b]
        spot = [jnp.where(j < n, nbr[b, j] - first, -1) for j in range(nnb)]
        tiles = [blk[b, j] for j in range(nnb)]
        there = pl.ds(pl.multiple_of(b * bs, bs), bs)
        for s in range(nb + 2):
            total = jnp.zeros((bs, bs), BF16)
            for j in range(nnb):
                weight = jnp.where(spot[j] == s, 1.0, 0.0).astype(F32)
                total = total + tiles[j] * jnp.full((bs, bs), weight, F32).astype(BF16)
            if s == 0:
                mat_halo[there, 0:bs] = total
            elif s == nb + 1:
                mat_halo[there, bs:2 * bs] = total
            else:
                mat_in[there, (s - 1) * bs:s * bs] = total


    step = min(rows, 2 * bs)

    @pl.loop(0, rows // step)
    def _(i):
        there = pl.ds(pl.multiple_of(i * step, step), step)
        inside = dot(mat_in[there, :], own[...])
        acc[there, :] = inside
        image[there, :] = inside.astype(BF16)

    for side in range(2):
        reach[side] = dot(bt[side], mat_halo[...]).astype(BF16)
    for u in proj:
        ready[u - PARTS] = dot(bt[1 - c], image[:, columns(u)])
    for u in proj:
        half[u] = dot(bt[c], image[:, columns(u)])

    for copy in halo_copies:
        copy.wait_recv()

    proj_core = [
        core_phase(u, ready[u - PARTS] + dot(reach[1 - c], halo[:, columns(u)])) for u in proj
    ]
    gram_line = [line_phase(u, gram_plane[u]) for u in gram]
    for u in proj:
        half[u] += dot(reach[c], halo[:, columns(u)])
    proj_plane = [plane_phase(u, copy) for u, copy in zip(proj, proj_core)]
    get_vals.wait()

    sq_own[...] = jnp.zeros_like(sq_own)

    def rotate(i):
        there = pl.ds(pl.multiple_of(i * step, step), step)
        outside = dot(mat_halo[there, :], halo[...])
        full = dot((acc[there, :] + outside).astype(BF16), rot[...])
        rimg_v[there, :] = full.astype(BF16)
        resid = full - vals[...] * rfull[there, :]
        sq_own[...] += fold(resid * resid)

    middle = rows // step // 2
    pl.loop(0, middle)(rotate)
    gram_gather = [gather_phase(u, gram_line[u]) for u in gram]
    pl.loop(middle, rows // step)(rotate)

    sq_copy = remote(sq_own, sq_core, core_ss.at[SQ], core_rs.at[SQ], mate)

    proj_line = [line_phase(u, copies) for u, copies in zip(proj, proj_plane)]
    sq_copy.wait_recv()
    sq_plane[q] = sq_own[...] + sq_core[...]
    sq_copies = [
        remote(sq_plane.at[q], sq_plane.at[q], plane_ss.at[SQ, d], plane_rs.at[SQ, d], plane[d])
        for d in range(Q - 1)
    ]
    for u in gram:
        finish(u, gram_gather[u])
    proj_gather = [gather_phase(u, copies) for u, copies in zip(proj, proj_line)]
    for copy in sq_copies:
        copy.wait_recv()
    sq_z[z] = jnp.sum(sq_plane[...], axis=0)
    sq_copies = [
        remote(sq_z.at[z], sq_z.at[z], za_ss.at[SQ, d], za_rs.at[SQ, d], line[d])
        for d in range(Z - 1)
    ]
    for u, copies in zip(proj, proj_gather):
        finish(u, copies)
    for copy in sq_copies:
        copy.wait_recv()
    squares = jnp.sum(jnp.sum(sq_z[...], axis=0), axis=0, keepdims=True)
    res_out[...] = jnp.sqrt(squares / rows_total)
    for copy in sends:
        copy.wait_send()


def fused_body(basis, blocks, neighbours, counts, rotation, ritz_values):
    R, Z = lax.axis_size("rows"), lax.axis_size("cols")
    nb, nnb, bs, _ = blocks.shape
    rows, k = basis.shape
    m = rotation.shape[1]
    Q, chunk, piece, wide = R // 2, k // R, k // R // Z, k // PARTS
    vmem = pltpu.VMEM
    dma = pltpu.SemaphoreType.DMA
    hbm_spec = pl.BlockSpec(memory_space=pltpu.HBM)
    vmem_spec = pl.BlockSpec(memory_space=pltpu.VMEM)
    ritz, rimg, sums, res = pl.pallas_call(
        functools.partial(kernel, (nb, nnb, bs, k, m, R, Z)),
        out_shape=(
            jax.ShapeDtypeStruct((rows, m), BF16),
            jax.ShapeDtypeStruct((rows, m), BF16),
            jax.ShapeDtypeStruct((2, chunk, k), F32),
            jax.ShapeDtypeStruct((1, m), F32),
        ),
        in_specs=[hbm_spec] * 6,
        out_specs=(vmem_spec,) * 4,
        scratch_shapes=[
            pltpu.SMEM((nb, nnb), jnp.int32),
            pltpu.SMEM((1, nb), jnp.int32),
            vmem((k, m), BF16),
            vmem((1, m), F32),
            vmem((rows, k), BF16),
            vmem((nb, nnb, bs, bs), BF16),
            vmem((rows, nb * bs), BF16),
            vmem((rows, 2 * bs), BF16),
            vmem((2 * bs, k), BF16),
            vmem((rows, k), F32),
            vmem((rows, k), BF16),
            vmem((2, k // 2, rows), BF16),
            vmem((rows, m), F32),
            vmem((2, k // 2, 2 * bs), BF16),
            vmem((PARTS, k // 2, wide), F32),
            vmem((SQ, k // 2, wide), F32),
            vmem((SQ, k // 2, wide), BF16),
            vmem((SQ, k // 2, wide), BF16),
            vmem((SQ, chunk, wide), F32),
            vmem((SQ, Q, chunk, wide), BF16),
            vmem((SQ, Q - 1, chunk, wide), BF16),
            vmem((SQ, Z, piece, wide), BF16),
            vmem((SQ, Z - 1, piece, wide), BF16),
            vmem((SQ, Z, piece, wide), BF16),
            vmem((8, m), F32),
            vmem((8, m), F32),
            vmem((Q, 8, m), F32),
            vmem((Z, 8, m), F32),
            dma((6,)),
            dma((2,)),
            dma((2,)),
            dma((SQ + 1,)),
            dma((SQ + 1,)),
            dma((SQ + 1, Q - 1)),
            dma((SQ + 1, Q - 1)),
            dma((SQ, Z - 1)),
            dma((SQ, Z - 1)),
            dma((SQ + 1, Z - 1)),
            dma((SQ + 1, Z - 1)),
        ],
        compiler_params=pltpu.CompilerParams(
            collective_id=0, has_side_effects=True, vmem_limit_bytes=36 * 1024 * 1024
        ),
        name="davidson_step",
    )(*[
        pltpu.with_memory_space_constraint(x, pltpu.HBM)
        for x in (neighbours, counts.reshape(1, nb), basis, blocks, rotation,
                  ritz_values.reshape(1, m))
    ])
    return ritz, rimg, sums[0], sums[1], res.reshape(m)


def body(basis, blocks, neighbours, counts, rotation, ritz_values):
    R, Z = lax.axis_size("rows"), lax.axis_size("cols")
    k = basis.shape[1]
    even = R % 4 == 0 and Z > 1 and k % (16 * R * Z) == 0 and (2 * k // R) % 128 == 0
    chosen = fused_body if even else general_body
    return chosen(basis, blocks, neighbours, counts, rotation, ritz_values)


def solution(mesh):
    return jax.shard_map(
        body,
        mesh=mesh,
        in_specs=(
            P(("rows", "cols"), None),
            P(("rows", "cols"), None, None, None),
            P(("rows", "cols"), None),
            P(("rows", "cols")),
            P(),
            P(),
        ),
        out_specs=(
            P(("rows", "cols"), None),
            P(("rows", "cols"), None),
            P("rows", None),
            P("rows", None),
            P(),
        ),
        check_vma=False,
    )
```
